1024 devices in a mesh: lon: 32 (over x_lo, y, core), lat: 32 (over x_hi, z).
Axes of the slice: x: 8 (x_hi: 4, x_lo: 2; x = x_hi * 2 + x_lo), y: 8, z: 8, core: 2. Of those that a mesh axis runs over, the one named last changes fastest.
Arguments:
- adjoint_in: float32 [384, 384, 216], P('lat', 'lon'), may hold values from -6 to 6
- stored_winds: bfloat16 [4, 384, 384, 144], P(None, 'lat', 'lon'), may hold values from -0.34 to 0.34
- innovations: bfloat16 [32, 32, 256, 216], P('lat', 'lon'), may hold values from -6 to 6
- columns: int32 [32, 32, 256], P('lat', 'lon'), may hold values from 0 to 143
- kernel_ids: int32 [32, 32, 256], P('lat', 'lon'), may hold values from 0 to 63
- counts: int32 [32, 32, 32], P('lat', 'lon'), may hold values from 0 to 8, as said below
- offsets: int32 [32, 32, 32], P('lat', 'lon'), may hold values from 0 to 248, as said below
- kernel_table: float32 [64, 216], replicated, may hold values from 0.1 to 1.5
- correlation: bfloat16 [384, 384], P(None, 'lon'), may hold values from -0.3125 to 0.3125
Outputs:
- adjoint_field: float32 [384, 384, 216], P('lat', 'lon')
- flux_gradient: float32 [384, 3, 384], P('lat', None, 'lon')
The draws below stay inside these ranges and needn't reach their ends.
Inputs may be any that keep to these rules, and one draw needn't show every extreme that they name: For each device and owner, the rows offsets to offsets + counts - 1 form that owner's run; the runs are disjoint, in owner order, and lie within the 256 rows. In every band some owner receives exactly 8 rows from every device of the band. `offsets`: start of each owner's run, as described for counts.
All inputs are finite; a program needn't handle non-finite values.
Results may differ from the reference program's by a relative error of at most 0.0029.
Values may be sent and summed in bfloat16 or wider, within the bound.
No kernel may reach another device: no remote copies, remote signals or barrier semaphores. Data moves between devices by JAX's collectives and lax.ppermute only.
A program may use at most 32 MiB of HBM per device.

```python
import jax
import jax.numpy as jnp
from jax import lax

SPECIES = 3
LEVELS = 72
STEPS = 4
KERNELS = 64
CLAT = 12
CLON = 12
CAP = 8
LAT_DEVS = 32
LON_DEVS = 32
NLAT = 384
NLON = 384
CELLS = 144
ROWS_DEV = 256


def routing_plan(key):
    key_base, key_hot, key_gap = jax.random.split(key, 3)
    shape = (LAT_DEVS, LON_DEVS, LON_DEVS)
    base_counts = jax.random.randint(key_base, shape, 0, CAP // 2 + 1)
    hot_dest = jax.random.randint(key_hot, (LAT_DEVS,), 0, LON_DEVS)
    is_hot = jnp.arange(LON_DEVS)[None, None, :] == hot_dest[:, None, None]
    count_arr = jnp.where(is_hot, CAP, base_counts)
    gap_arr = jax.random.randint(key_gap, shape, 0, CAP // 4 + 1)
    first_owner = jnp.arange(LON_DEVS)[None, None, :] == 0
    gap_arr = jnp.where(first_owner, 0, gap_arr)
    offset_arr = jnp.cumsum(count_arr + gap_arr, axis=-1) - count_arr
    last_owner = jnp.arange(LON_DEVS)[None, None, :] == LON_DEVS - 1
    offset_arr = jnp.where(last_owner, ROWS_DEV - CAP, offset_arr)
    return (count_arr.astype(jnp.int32), offset_arr.astype(jnp.int32))


def draw_counts(key, part):
    plan = routing_plan(key)
    return plan[0]


def draw_offsets(key, part):
    plan = routing_plan(key)
    return plan[1]


def draw_stored_winds(key, part):
    key = jax.random.fold_in(key, 3)
    key_sign, key_size = jax.random.split(key, 2)
    sign_bits = jax.random.randint(key_sign, (2 * LEVELS,), 0, 2)
    signs = jnp.where(sign_bits == 1, 1.0, -1.0).astype(jnp.float32)
    shape = (STEPS, NLAT, NLON, 2 * LEVELS)
    magnitude = jax.random.uniform(key_size, shape, jnp.float32, 0.17, 0.34)
    return (signs * magnitude).astype(jnp.bfloat16)


def with_ends(values, key, least, largest):
    place = [jax.random.randint(jax.random.fold_in(key, axis), (), 0, length) for axis, length in enumerate(values.shape)]
    longest = values.shape.index(max(values.shape))
    neighbour = place[:longest] + [(place[longest] + 1) % values.shape[longest]] + place[longest + 1:]
    return values.at[tuple(place)].set(least).at[tuple(neighbour)].set(largest)


def level_of(stream_key, shape, cuts, low, top_value):
    loudness, own = 1.0, jax.random.fold_in(stream_key, 6)
    for dim, parts in cuts:
        heights = jnp.exp(jax.random.uniform(jax.random.fold_in(own, dim), (parts,), jnp.float32, low / len(cuts), top_value / len(cuts)))
        loudness = loudness * jnp.repeat(heights, shape[dim] // parts).reshape([-1 if axis == dim else 1 for axis in range(len(shape))])
    return loudness


def bell_draw(stream_key, dims, deviation, most, cuts=(), held_as=jnp.bfloat16):
    entries = jax.random.normal(stream_key, dims, jnp.float32) * deviation
    if len(cuts) > 0:
        entries = level_of(stream_key, dims, cuts, -0.22, 0.18) * entries
    return jnp.clip(entries, min=-most, max=most).astype(held_as)


def setup_inputs(seed: int = 0) -> dict:
    streams_of = jax.random.split(jax.random.key(seed), 10)
    return {
        "adjoint_in": bell_draw(streams_of[0], (NLAT, NLON, SPECIES * LEVELS), 1.0, 6.0, ((0, 32), (1, 32)), jnp.float32),
        "stored_winds": draw_stored_winds(jax.random.fold_in(streams_of[9], 71), 0),
        "innovations": bell_draw(streams_of[2], (LAT_DEVS, LON_DEVS, ROWS_DEV, SPECIES * LEVELS), 1.0, 6.0, ((0, 32), (1, 32))),
        "columns": with_ends(jax.random.randint(streams_of[3], (LAT_DEVS, LON_DEVS, ROWS_DEV), 0, CELLS), jax.random.fold_in(streams_of[3], 1), 0, CELLS - 1).astype(jnp.int32),
        "kernel_ids": with_ends(jax.random.randint(streams_of[4], (LAT_DEVS, LON_DEVS, ROWS_DEV), 0, KERNELS), jax.random.fold_in(streams_of[4], 1), 0, KERNELS - 1).astype(jnp.int32),
        "counts": draw_counts(jax.random.fold_in(streams_of[9], 71), 0),
        "offsets": draw_offsets(jax.random.fold_in(streams_of[9], 71), 0),
        "kernel_table": jnp.clip(jax.random.uniform(streams_of[7], (KERNELS, SPECIES * LEVELS), jnp.float32, 0.1, 1.5), 0.1, 1.5),
        "correlation": bell_draw(streams_of[8], (NLON, NLON), NLON ** -0.5, 0.3125, ((1, 32),)),
    }


HORIZ_MIX = 0.18
VERT_MIX = 0.1


def advance(center, east, west, north, south, east_wind, north_wind):
    levels = east_wind.shape[-1]
    shaped = center.shape[:-1] + (center.shape[-1] // levels, levels)
    middle = center.reshape(shaped)
    east_v = east.reshape(shaped)
    west_v = west.reshape(shaped)
    north_v = north.reshape(shaped)
    south_v = south.reshape(shaped)
    upper = jnp.concatenate([middle[..., 1:], middle[..., -1:]], axis=-1)
    lower = jnp.concatenate([middle[..., :1], middle[..., :-1]], axis=-1)
    east_c = east_wind[..., None, :]
    north_c = north_wind[..., None, :]
    result = (middle + east_c * (east_v - west_v) * 0.5 + north_c * (north_v - south_v) * 0.5
              + HORIZ_MIX * (east_v + west_v + north_v + south_v - 4.0 * middle)
              + VERT_MIX * (upper + lower - 2.0 * middle))
    return result.reshape(center.shape)


def reference(adjoint_in, stored_winds, innovations, columns, kernel_ids, counts, offsets, kernel_table, correlation):
    width = SPECIES * LEVELS
    row_ids = jnp.arange(ROWS_DEV, dtype=jnp.int32)
    owner_ids = jnp.arange(LON_DEVS, dtype=jnp.int32)
    inrun = (offsets[:, :, None, :] <= row_ids[None, None, :, None]) & (
        row_ids[None, None, :, None] < (offsets + counts)[:, :, None, :])
    owner = jnp.sum(jnp.where(inrun, owner_ids[None, None, None, :], 0), axis=-1).astype(jnp.int32)
    used = jnp.any(inrun, axis=-1)
    bands = jnp.arange(LAT_DEVS, dtype=jnp.int32)[:, None, None]
    glat = bands * CLAT + columns // CLON
    glon = owner * CLON + columns % CLON
    flat = jnp.where(used, glat * NLON + glon, NLAT * NLON).astype(jnp.int32)
    onehot = (kernel_ids[..., None] == jnp.arange(KERNELS, dtype=jnp.int32)).astype(jnp.float32)
    table_rows = jnp.einsum("berk,kf->berf", onehot, kernel_table, precision=lax.Precision.HIGHEST)
    weighted = innovations.astype(jnp.float32) * table_rows
    forcing = jnp.zeros((NLAT * NLON, width), jnp.float32).at[flat.reshape(-1)].add(
        weighted.reshape(-1, width), mode="drop").reshape(NLAT, NLON, width)
    field = adjoint_in + forcing
    surface = jnp.zeros((NLAT, NLON, SPECIES), jnp.float32)
    for step_index in range(STEPS):
        winds_now = stored_winds[STEPS - 1 - step_index].astype(jnp.float32)
        east_wind = winds_now[..., :LEVELS]
        north_wind = winds_now[..., LEVELS:]
        pieces = []
        for species in range(SPECIES):
            part_field = field[..., species * LEVELS:(species + 1) * LEVELS]
            east = jnp.roll(part_field, -1, axis=1)
            west = jnp.roll(part_field, 1, axis=1)
            zero_row = jnp.zeros_like(part_field[:1])
            north = jnp.concatenate([part_field[1:], zero_row], axis=0)
            south = jnp.concatenate([zero_row, part_field[:-1]], axis=0)
            pieces.append(advance(part_field, east, west, north, south, east_wind, north_wind))
        field = jnp.concatenate(pieces, axis=-1)
        surface = surface + field[..., ::LEVELS]
    surface_bf = jnp.transpose(surface.astype(jnp.bfloat16), (0, 2, 1)).reshape(NLAT * SPECIES, NLON)
    gradient = jnp.dot(surface_bf, correlation, preferred_element_type=jnp.float32)
    return field, gradient.reshape(NLAT, SPECIES, NLON)
```

```python
import functools

import jax
import jax.numpy as jnp
from jax import lax
from jax.experimental import pallas as pl
from jax.experimental.pallas import tpu as pltpu
from jax.sharding import PartitionSpec as P

CAP = 8
HORIZ_MIX = 0.18
VERT_MIX = 0.1
CENTER = 1.0 - 4.0 * HORIZ_MIX - 2.0 * VERT_MIX

ROWS = 12
HALO = 4
SUB = 16
WIDE = 256
LEVELS = 72
SPECIES = 3
WIDTH = SPECIES * LEVELS
CODE_LANE = 216
KERNEL_LANE = 217
F32 = jnp.float32
BF16 = jnp.bfloat16


def iota(shape, dim):
    return lax.broadcasted_iota(jnp.int32, shape, dim)


def vmem_call(body, outs, scratch=(), name=None):
    return pl.pallas_call(
        body,
        out_shape=outs,
        scratch_shapes=list(scratch),
        name=name,
        compiler_params=pltpu.CompilerParams(vmem_limit_bytes=48 * 1024 * 1024),
    )


def split2(value):
    high = value.astype(BF16).astype(F32)
    return high, (value - high).astype(BF16).astype(F32)


def route_body(innov_ref, columns_ref, kernels_ref, counts_ref, offsets_ref, out_ref, padded_ref):
    held = innov_ref.shape[2]
    owners = counts_ref.shape[2]
    eye = iota((owners, owners), 0) == iota((owners, owners), 1)
    offset_col = jnp.sum(jnp.where(eye, offsets_ref[0].astype(F32), 0.0), axis=1, keepdims=True)
    count_col = jnp.sum(jnp.where(eye, counts_ref[0].astype(F32), 0.0), axis=1, keepdims=True)
    place = iota((owners, held), 1).astype(F32) - offset_col
    place = jnp.where(place < count_col, place, -1.0)
    slot = iota((owners, CAP, held), 1).astype(F32)
    pick = jnp.where(place[:, None, :] == slot, 1.0, 0.0).reshape(owners * CAP, held).astype(BF16)
    padded_ref[...] = jnp.zeros_like(padded_ref)
    padded_ref[:, :WIDTH] = innov_ref[0, 0]
    cell = columns_ref[0]
    code = (cell + 4 * ((cell * 171) >> 11) + 1).astype(F32)
    half = WIDE // 2
    line = iota((half, held), 0)
    codes = jnp.where(
        line == CODE_LANE - half,
        code,
        jnp.where(line == KERNEL_LANE - half, kernels_ref[0].astype(F32), 0.0),
    ).astype(BF16)
    sent = jnp.dot(pick, padded_ref[...], preferred_element_type=F32)
    tail = lax.dot_general(pick, codes, (((1,), (1,)), ((), ())), preferred_element_type=F32)
    out_ref[:, :half] = sent[:, :half].astype(BF16)
    out_ref[:, half:] = (sent[:, half:] + tail).astype(BF16)


def pad_winds_body(winds_ref, out_ref):
    out_ref[...] = jnp.zeros_like(out_ref)
    out_ref[:, :, :ROWS, : 2 * LEVELS] = winds_ref[...]


def force_body(recv_ref, table_ref, adjoint_ref, winds_ref, lam_ref, north_ref, south_ref, table_s):
    total = recv_ref.shape[0]
    nkernel = table_ref.shape[0]
    recv = recv_ref[...]
    wide = recv.astype(F32)
    pick = jnp.where((iota((8, WIDE), 1) == CODE_LANE), 1.0, 0.0).astype(BF16)
    code_line = lax.dot_general(pick, recv, (((1,), (1,)), ((), ())), preferred_element_type=F32)
    kernel_col = wide[:, KERNEL_LANE : KERNEL_LANE + 1]
    lane = iota((total, 3 * nkernel), 1)
    lane = (lane - jnp.where(lane >= nkernel, nkernel, 0) - jnp.where(lane >= 2 * nkernel, nkernel, 0)).astype(F32)
    onehot = jnp.where(kernel_col == lane, 1.0, 0.0).astype(BF16)
    table = table_ref[...]
    table_s[...] = jnp.zeros_like(table_s)
    high = table.astype(BF16)
    rest = table - high.astype(F32)
    middle = rest.astype(BF16)
    table_s[0:nkernel, :WIDTH] = high
    table_s[nkernel : 2 * nkernel, :WIDTH] = middle
    table_s[2 * nkernel :, :WIDTH] = (rest - middle.astype(F32)).astype(BF16)
    weights = jnp.dot(onehot, table_s[...], preferred_element_type=F32)
    weighted = wide * weights
    whigh = weighted.astype(BF16)
    wlow = (weighted - whigh.astype(F32)).astype(BF16)
    cell = (iota((ROWS * SUB, total), 0) + 1).astype(F32)
    scatter = jnp.where(cell == code_line[0:1, :], 1.0, 0.0).astype(BF16)
    force = jnp.dot(scatter, whigh, preferred_element_type=F32) + jnp.dot(
        scatter, wlow, preferred_element_type=F32
    )
    lam_ref[...] = force.reshape(ROWS, SUB, WIDE)
    lam_ref[:, :ROWS, :WIDTH] = lam_ref[:, :ROWS, :WIDTH] + adjoint_ref[...]
    for strip, first in ((north_ref, ROWS - HALO), (south_ref, 0)):
        edge = lam_ref[first : first + HALO]
        ehigh = edge.astype(BF16)
        strip[0:4] = ehigh
        strip[4:8] = (edge - ehigh.astype(F32)).astype(BF16)
        base = 8
        for step in (1, 2, 3):
            depth = HALO - step
            start = ROWS - depth if first else 0
            strip[base : base + depth] = winds_ref[4 - step, start : start + depth]
            base += depth


WIND_BASE = {1: 8, 2: 11, 3: 13}


def ext_lam(lam_ref, from_north, from_south, row):
    if 0 <= row < ROWS:
        return lam_ref[row]
    strip, index = (from_north, row - ROWS) if row >= ROWS else (from_south, row + HALO)
    return strip[index].astype(F32) + strip[index + 4].astype(F32)


def ext_wind(winds_ref, from_north, from_south, step, row):
    if 0 <= row < ROWS:
        return winds_ref[4 - step, row].astype(F32)
    depth = HALO - step
    if row >= ROWS:
        strip, index = from_north, row - ROWS
    else:
        strip, index = from_south, row + depth
    if not 0 <= index < depth:
        return jnp.zeros((SUB, WIDE), F32)
    return strip[WIND_BASE[step] + index].astype(F32)


def ext_index(row):
    return row if row >= 0 else row + ROWS + 2 * HALO


def edge_body(lam_ref, from_north, from_south, winds_ref, east_ref, west_ref):
    sub = iota((8, WIDE), 0)
    for row in range(-HALO, ROWS + HALO):
        lam = ext_lam(lam_ref, from_north, from_south, row)
        w1 = ext_wind(winds_ref, from_north, from_south, 1, row)
        w2 = ext_wind(winds_ref, from_north, from_south, 2, row)
        w3 = ext_wind(winds_ref, from_north, from_south, 3, row)
        for out, tile in ((east_ref, 1), (west_ref, 0)):
            cut = slice(8 * tile, 8 * tile + 8)
            high, low = split2(lam[cut])
            values = jnp.where(sub < 4, high, pltpu.roll(low, 4, 0))
            first = pltpu.roll(w1[cut], 4, 0)
            if tile == 1:
                rest = jnp.where(sub >= 2, w2[cut], pltpu.roll(w3[cut], 6, 0))
            else:
                rest = jnp.where(sub < 2, w2[cut], pltpu.roll(w3[cut], 2, 0))
            winds = jnp.where(sub >= 4, first, rest)
            out[ext_index(row)] = jnp.concatenate([values, winds], axis=0).astype(BF16)


def steps_body(
    lam_ref, from_north, from_south, winds_ref, from_east, from_west, field_ref, surface_ref,
    lam_a, lam_b, wide_s, coef_s, acc_s,
):
    lat = lax.axis_index("lat")
    has_south = jnp.where(lat > 0, 1.0, 0.0).astype(F32)
    has_north = jnp.where(lat < lax.axis_size("lat") - 1, 1.0, 0.0).astype(F32)
    cols = SUB + 8
    sub = iota((8, WIDE), 0)
    for row in range(-HALO, ROWS + HALO):
        at = ext_index(row)
        lam = ext_lam(lam_ref, from_north, from_south, row)
        east = from_east[at].astype(F32)
        west = from_west[at].astype(F32)
        east_lam = east[0:8] + pltpu.roll(east[0:8], 4, 0)
        west_lam = west[0:8] + pltpu.roll(west[0:8], 4, 0)
        lam_a[at, 0:8] = lam[0:8]
        lam_a[at, 8:16] = jnp.where(sub < 4, lam[8:16], east_lam)
        lam_a[at, 16:24] = west_lam
        for step in range(1, 5):
            reach = HALO - step
            if not -reach <= row < ROWS + reach:
                continue
            wind = ext_wind(winds_ref, from_north, from_south, step, row)
            ew, ww = east[8:16], west[8:16]
            if step == 2:
                ew, ww = pltpu.roll(ew, 4, 0), pltpu.roll(ww, 4, 0)
            if step == 3:
                ew, ww = pltpu.roll(ew, 2, 0), pltpu.roll(ww, 6, 0)
            place = (step - 1) * (ROWS + 2 * HALO) + at
            wide_s[place, 0:16] = jnp.concatenate(
                [wind[0:8], jnp.where(sub < 4, wind[8:16], ew)], axis=0
            ).astype(BF16)
            wide_s[place, 16:24] = ww.astype(BF16)
    spread_k = iota((WIDE, 2 * WIDE), 0)
    spread_n = iota((WIDE, 2 * WIDE), 1)
    north_half = spread_n >= WIDE
    lane_n = jnp.where(north_half, spread_n - WIDE, spread_n)
    level_n = lane_n - jnp.where(lane_n >= LEVELS, LEVELS, 0) - jnp.where(lane_n >= 2 * LEVELS, LEVELS, 0)
    match = (spread_k == level_n + jnp.where(north_half, LEVELS, 0)) & (lane_n < WIDTH)
    spread = jnp.where(match, 0.5, 0.0).astype(BF16)
    lane = iota((cols, WIDE), 1)
    top = (lane == LEVELS - 1) | (lane == 2 * LEVELS - 1) | (lane == 3 * LEVELS - 1)
    bottom = (lane == 0) | (lane == LEVELS) | (lane == 2 * LEVELS)
    now, later = lam_a, lam_b
    for step in range(1, 5):
        reach = HALO - step
        rows = list(range(-reach, ROWS + reach))
        order = sorted(ext_index(r) for r in rows)
        groups = [(0, ROWS + reach)]
        if reach:
            groups.append((ROWS + 2 * HALO - reach, ROWS + 2 * HALO))
        base = (step - 1) * (ROWS + 2 * HALO)
        for lo, hi in groups:
            lhs = wide_s[base + lo : base + hi].reshape((hi - lo) * cols, WIDE)
            coef_s[lo:hi] = jnp.dot(lhs, spread, preferred_element_type=F32).reshape(hi - lo, cols, 2 * WIDE)
        del order
        for row in rows:
            at = ext_index(row)
            mid = now[at]
            north = now[ext_index(row + 1)]
            south = now[ext_index(row - 1)]
            east = pltpu.roll(mid, cols - 1, 0)
            west = pltpu.roll(mid, 1, 0)
            upper = jnp.where(top, mid, pltpu.roll(mid, WIDE - 1, 1))
            lower = jnp.where(bottom, mid, pltpu.roll(mid, 1, 1))
            u = coef_s[at, :, :WIDE]
            v = coef_s[at, :, WIDE:]
            new = (
                CENTER * mid
                + u * (east - west)
                + v * (north - south)
                + HORIZ_MIX * ((east + west) + (north + south))
                + VERT_MIX * (upper + lower)
            )
            if row < 0:
                new = new * has_south
            if row >= ROWS:
                new = new * has_north
            if step < 4:
                later[at] = new
            else:
                field_ref[row] = new[:ROWS, :WIDTH]
            if 0 <= row < ROWS:
                if step == 1:
                    acc_s[row] = new[:SUB]
                else:
                    acc_s[row] = acc_s[row] + new[:SUB]
        now, later = later, now
    lane = iota((SUB, 128), 1)
    surface = jnp.zeros((SUB, 128), F32)
    for row in range(ROWS):
        for species in range(SPECIES):
            at = row * SPECIES + species
            source = species * LEVELS
            half = acc_s[row][:, 128 * (source // 128) : 128 * (source // 128) + 128]
            moved = pltpu.roll(half, (at - source % 128) % 128, 1)
            surface = jnp.where(lane == at, moved, surface)
    surface = jnp.where(iota((SUB, 128), 0) < ROWS, surface, 0.0).astype(BF16)
    for target in range(surface_ref.shape[0]):
        surface_ref[target] = surface


def pad_correlation_body(correlation_ref, out_ref):
    total, mine = correlation_ref.shape
    out_ref[...] = jnp.zeros_like(out_ref)
    for block in range(total // ROWS):
        out_ref[block, :ROWS, :mine] = correlation_ref[block * ROWS : block * ROWS + ROWS]


def gradient_body(surface_ref, correlation_ref, out_ref):
    blocks = surface_ref.shape[0]
    surface = surface_ref[...].reshape(blocks * SUB, 128)
    correlation = correlation_ref[...].reshape(blocks * SUB, 128)
    result = lax.dot_general(surface, correlation, (((0,), (0,)), ((), ())), preferred_element_type=F32)
    for row in range(ROWS):
        out_ref[row] = result[SPECIES * row : SPECIES * row + SPECIES, :ROWS]


def per_device(
    adjoint_in, stored_winds, innovations, columns, kernel_ids, counts, offsets, kernel_table, correlation
):
    lon_count = lax.axis_size("lon")
    lat_count = lax.axis_size("lat")
    shape = jax.ShapeDtypeStruct
    sent = vmem_call(
        route_body,
        shape((lon_count * CAP, WIDE), BF16),
        [pltpu.VMEM((innovations.shape[2], WIDE), BF16)],
        name="route",
    )(innovations, columns, kernel_ids, counts, offsets)
    recv = lax.all_to_all(sent, "lon", split_axis=0, concat_axis=0, tiled=True)
    winds = vmem_call(pad_winds_body, shape((4, ROWS, SUB, WIDE), BF16), name="pad_winds")(stored_winds)
    spread = vmem_call(pad_correlation_body, shape((lon_count, SUB, 128), BF16), name="pad_correlation")(correlation)
    strip = shape((14, SUB, WIDE), BF16)
    lam, north, south = vmem_call(
        force_body,
        (shape((ROWS, SUB, WIDE), F32), strip, strip),
        [pltpu.VMEM((3 * kernel_table.shape[0], WIDE), BF16)],
        name="force",
    )(recv, kernel_table, adjoint_in, winds)
    up = [(i, i + 1) for i in range(lat_count - 1)]
    down = [(i + 1, i) for i in range(lat_count - 1)]
    from_south = lax.ppermute(north, "lat", up)
    from_north = lax.ppermute(south, "lat", down)
    edge = shape((ROWS + 2 * HALO, SUB, WIDE), BF16)
    east, west = vmem_call(edge_body, (edge, edge), name="edge")(lam, from_north, from_south, winds)
    forward = [(i, (i + 1) % lon_count) for i in range(lon_count)]
    backward = [((i + 1) % lon_count, i) for i in range(lon_count)]
    from_west = lax.ppermute(east, "lon", forward)
    from_east = lax.ppermute(west, "lon", backward)
    ext = ROWS + 2 * HALO
    cols = SUB + 8
    field, surface = vmem_call(
        steps_body,
        (shape((ROWS, ROWS, WIDTH), F32), shape((lon_count, SUB, 128), BF16)),
        [
            pltpu.VMEM((ext, cols, WIDE), F32),
            pltpu.VMEM((ext, cols, WIDE), F32),
            pltpu.VMEM((4 * ext, cols, WIDE), BF16),
            pltpu.VMEM((ext, cols, 2 * WIDE), F32),
            pltpu.VMEM((ROWS, SUB, WIDE), F32),
        ],
        name="steps",
    )(lam, from_north, from_south, winds, from_east, from_west)
    gathered = lax.all_to_all(surface, "lon", split_axis=0, concat_axis=0, tiled=True)
    gradient = vmem_call(gradient_body, shape((ROWS, SPECIES, ROWS), F32), name="gradient")(gathered, spread)
    return field, gradient


def solution(mesh):
    return jax.shard_map(
        per_device,
        mesh=mesh,
        in_specs=(
            P("lat", "lon", None),
            P(None, "lat", "lon", None),
            P("lat", "lon", None, None),
            P("lat", "lon", None),
            P("lat", "lon", None),
            P("lat", "lon", None),
            P("lat", "lon", None),
            P(),
            P(None, "lon"),
        ),
        out_specs=(P("lat", "lon", None), P("lat", None, "lon")),
        check_vma=False,
    )
```

```python
import functools

import jax
import jax.numpy as jnp
from jax import lax
from jax.experimental import pallas as pl
from jax.experimental.pallas import tpu as pltpu
from jax.sharding import PartitionSpec as P

CAP = 8
HORIZ_MIX = 0.18
VERT_MIX = 0.1
CENTER = 1.0 - 4.0 * HORIZ_MIX - 2.0 * VERT_MIX

ROWS = 12
HALO = 4
SUB = 16
WIDE = 256
LEVELS = 72
SPECIES = 3
WIDTH = SPECIES * LEVELS
CODE_LANE = 216
KERNEL_LANE = 217
F32 = jnp.float32
BF16 = jnp.bfloat16


def iota(shape, dim):
    return lax.broadcasted_iota(jnp.int32, shape, dim)


def vmem_call(body, outs, scratch=(), name=None, limit=48 * 1024 * 1024, **specs):
    return pl.pallas_call(
        body,
        out_shape=outs,
        scratch_shapes=list(scratch),
        name=name,
        compiler_params=pltpu.CompilerParams(vmem_limit_bytes=limit),
        **specs,
    )


def split2(value):
    high = value.astype(BF16).astype(F32)
    return high, (value - high).astype(BF16).astype(F32)


def route_body(
    counts_hbm, offsets_hbm, columns_hbm, kernels_hbm, innov_hbm, out_ref,
    counts_s, offsets_s, columns_s, kernels_s, innov_s, sems,
):
    moves = (
        (counts_hbm.at[0], counts_s),
        (offsets_hbm.at[0], offsets_s),
        (columns_hbm.at[0], columns_s),
        (kernels_hbm.at[0], kernels_s),
        (innov_hbm.at[0, 0], innov_s),
    )
    copies = [pltpu.make_async_copy(source, target, sems.at[i]) for i, (source, target) in enumerate(moves)]
    for copy in copies:
        copy.start()
    for copy in copies[:4]:
        copy.wait()
    held = innov_s.shape[1]
    owners = counts_s.shape[1]
    eye = iota((owners, owners), 0) == iota((owners, owners), 1)
    offset_col = jnp.sum(jnp.where(eye, offsets_s[...].astype(F32), 0.0), axis=1, keepdims=True)
    count_col = jnp.sum(jnp.where(eye, counts_s[...].astype(F32), 0.0), axis=1, keepdims=True)
    place = iota((owners, held), 1).astype(F32) - offset_col
    place = jnp.where(place < count_col, place, -1.0)
    slot = iota((owners, CAP, held), 1).astype(F32)
    pick = jnp.where(place[:, None, :] == slot, 1.0, 0.0).reshape(owners * CAP, held).astype(BF16)
    cell = columns_s[...]
    code = (cell + 4 * ((cell * 171) >> 11) + 1).astype(F32)
    half = WIDE // 2
    line = iota((half, held), 0)
    codes = jnp.where(
        line == CODE_LANE - half,
        code,
        jnp.where(line == KERNEL_LANE - half, kernels_s[...].astype(F32), 0.0),
    ).astype(BF16)
    tail = lax.dot_general(pick, codes, (((1,), (1,)), ((), ())), preferred_element_type=F32)
    out_ref[:, half:] = tail.astype(BF16)
    copies[4].wait()
    sent = lax.dot_general(
        pick, innov_s[...], (((1,), (1,)), ((), ())), preferred_element_type=F32
    ).astype(BF16)
    out_ref[:, :half] = sent[:, :half]
    out_ref[:, half:WIDTH] = sent[:, half:]


def pad_winds_body(winds_ref, out_ref):
    out_ref[...] = jnp.zeros_like(out_ref)
    out_ref[:, :, :ROWS, : 2 * LEVELS] = winds_ref[...]


STRIP = 17


def pieces(row):
    return pltpu.roll(row[0:8], 4, 0), row[0:8], pltpu.roll(row[8:16], 4, 0)


def with_piece(row, piece):
    sub = iota((8, row.shape[1]), 0)
    return jnp.concatenate([row[0:8], jnp.where(sub < 4, row[8:16], piece)], axis=0)


def pack_strip(lam_rows, wind_rows):
    parts = [split2(row) for row in lam_rows]
    rows = [high for high, _ in parts] + [low for _, low in parts]
    extra = pieces(rows[6]) + pieces(rows[7])
    lane = iota((SUB, 128), 1)
    halves = []
    for index in range(6):
        packed = with_piece(rows[index], extra[index])
        spare = pltpu.roll(wind_rows[index][:, 128:], WIDTH - 128, 1)
        halves += [packed[:, :128], jnp.where(lane < WIDTH - 128, packed[:, 128:], spare)]
    main = [row[:, :128] for row in wind_rows]
    extra = pieces(main[4])
    halves += [with_piece(main[index], extra[index]) for index in range(3)] + [main[3], main[5]]
    return halves


def unpack_strip(halves):
    lane = iota((SUB, 128), 1)
    sub = iota((8, WIDE), 0)
    tiles = [
        jnp.concatenate([halves[2 * i], jnp.where(lane < WIDTH - 128, halves[2 * i + 1], 0.0)], axis=1)
        for i in range(6)
    ]
    rows = list(tiles)
    for index in (0, 3):
        first, second, third = (tile[8:16] for tile in tiles[index : index + 3])
        rows.append(
            jnp.concatenate([jnp.where(sub < 4, pltpu.roll(first, 4, 0), second), pltpu.roll(third, 4, 0)], axis=0)
        )
    lam_rows = [rows[i] + rows[i + 4] for i in range(4)]
    main = [halves[12], halves[13], halves[14], halves[15], None, halves[16]]
    first, second, third = (half[8:16] for half in main[:3])
    main[4] = jnp.concatenate(
        [jnp.where(sub[:, :128] < 4, pltpu.roll(first, 4, 0), second), pltpu.roll(third, 4, 0)], axis=0
    )
    wind_rows = []
    for index in range(6):
        spare = pltpu.roll(halves[2 * index + 1], 256 - WIDTH, 1)
        wind_rows.append(jnp.concatenate([main[index], jnp.where(lane < 2 * LEVELS - 128, spare, 0.0)], axis=1))
    return lam_rows, wind_rows


def force_body(recv_ref, table_ref, adjoint_ref, winds_ref, lam_ref, first_ref, second_ref, table_s):
    total = recv_ref.shape[0]
    nkernel = table_ref.shape[0]
    recv = recv_ref[...]
    wide = recv.astype(F32)
    pick = jnp.where((iota((8, WIDE), 1) == CODE_LANE), 1.0, 0.0).astype(BF16)
    code_line = lax.dot_general(pick, recv, (((1,), (1,)), ((), ())), preferred_element_type=F32)
    kernel_col = wide[:, KERNEL_LANE : KERNEL_LANE + 1]
    lane = iota((total, 3 * nkernel), 1)
    lane = (lane - jnp.where(lane >= nkernel, nkernel, 0) - jnp.where(lane >= 2 * nkernel, nkernel, 0)).astype(F32)
    onehot = jnp.where(kernel_col == lane, 1.0, 0.0).astype(BF16)
    table = table_ref[...]
    table_s[...] = jnp.zeros_like(table_s)
    high = table.astype(BF16)
    rest = table - high.astype(F32)
    middle = rest.astype(BF16)
    table_s[0:nkernel, :WIDTH] = high
    table_s[nkernel : 2 * nkernel, :WIDTH] = middle
    table_s[2 * nkernel :, :WIDTH] = (rest - middle.astype(F32)).astype(BF16)
    weights = jnp.dot(onehot, table_s[...], preferred_element_type=F32)
    weighted = wide * weights
    whigh = weighted.astype(BF16)
    wlow = (weighted - whigh.astype(F32)).astype(BF16)
    cell = (iota((ROWS * SUB, total), 0) + 1).astype(F32)
    scatter = jnp.where(cell == code_line[0:1, :], 1.0, 0.0).astype(BF16)
    force = jnp.dot(scatter, whigh, preferred_element_type=F32) + jnp.dot(
        scatter, wlow, preferred_element_type=F32
    )
    lam_ref[...] = force.reshape(ROWS, SUB, WIDE)
    lam_ref[:, :ROWS, :WIDTH] = lam_ref[:, :ROWS, :WIDTH] + adjoint_ref[...]
    made = []
    for lower in (False, True):
        start = 0 if lower else ROWS - HALO
        wind_rows = []
        for step in (1, 2, 3):
            depth = HALO - step
            begin = 0 if lower else ROWS - depth
            wind_rows += [winds_ref[4 - step, begin + i].astype(F32) for i in range(depth)]
        made.append(pack_strip([lam_ref[start + i] for i in range(HALO)], wind_rows))
    even = lax.rem(lax.axis_index("lat"), 2) == 0
    for index, (north, south) in enumerate(zip(*made, strict=True)):
        first_ref[index] = jnp.where(even, north, south).astype(BF16)
        second_ref[index] = jnp.where(even, south, north).astype(BF16)


WIND_FIRST = {1: 0, 2: 3, 3: 5}
EXT = ROWS + 2 * HALO


def ext_index(row):
    return row if row >= 0 else row + EXT


def wind_index(step, row):
    base = (0, 18, 34, 48)[step - 1]
    reach = HALO - step
    return base + (row if row >= 0 else row + ROWS + 2 * reach)


def edge_body(lam_ref, from_first, from_second, winds_ref, sibling_ref, cross_ref, lam_out, winds_out):
    even_lat = lax.rem(lax.axis_index("lat"), 2) == 0
    first = [from_first[i].astype(F32) for i in range(STRIP)]
    second = [from_second[i].astype(F32) for i in range(STRIP)]
    north_lam, north_winds = unpack_strip([jnp.where(even_lat, a, b) for a, b in zip(first, second, strict=True)])
    south_lam, south_winds = unpack_strip([jnp.where(even_lat, b, a) for a, b in zip(first, second, strict=True)])
    even = lax.rem(lax.axis_index("lon"), 2) == 0
    sub = iota((8, WIDE), 0)
    none = jnp.zeros((SUB, WIDE), F32)
    for row in range(-HALO, ROWS + HALO):
        own = 0 <= row < ROWS
        lam = lam_ref[row] if own else (south_lam[row + HALO] if row < 0 else north_lam[row - ROWS])
        lam_out[ext_index(row)] = lam
        wind = {}
        for step in (1, 2, 3, 4):
            reach = HALO - step
            if own:
                raw = winds_ref[4 - step, row]
                winds_out[wind_index(step, row)] = raw
                wind[step] = raw.astype(F32)
            elif -reach <= row < ROWS + reach:
                rows, at = (south_winds, row + reach) if row < 0 else (north_winds, row - ROWS)
                wind[step] = rows[WIND_FIRST[step] + at]
                winds_out[wind_index(step, row)] = wind[step].astype(BF16)
            else:
                wind[step] = none
        made = []
        for tile in (1, 0):
            cut = slice(8 * tile, 8 * tile + 8)
            high, low = split2(lam[cut])
            values = jnp.where(sub < 4, high, pltpu.roll(low, 4, 0))
            upper = pltpu.roll(wind[1][cut], 4, 0)
            if tile == 1:
                rest = jnp.where(sub >= 2, wind[2][cut], pltpu.roll(wind[3][cut], 6, 0))
            else:
                rest = jnp.where(sub < 2, wind[2][cut], pltpu.roll(wind[3][cut], 2, 0))
            made.append(jnp.concatenate([values, jnp.where(sub >= 4, upper, rest)], axis=0))
        to_east, to_west = made
        sibling_ref[ext_index(row)] = jnp.where(even, to_east, to_west).astype(BF16)
        cross_ref[ext_index(row)] = jnp.where(even, to_west, to_east).astype(BF16)


def pack_low(tile):
    lane = iota(tile.shape[:-1] + (128,), len(tile.shape) - 1)
    return jnp.where((lane >= 16) & (lane < 24), tile[..., 128:], tile[..., :128])


def assemble(refs, lam_s, wide_s, narrow):
    lam_ref, winds_ref, from_sibling, from_cross = refs
    even = lax.rem(lax.axis_index("lon"), 2) == 0
    sub = iota((8, 128 if narrow else WIDE), 0)
    lanes = 128 if narrow else WIDE
    keep = pack_low if narrow else (lambda tile: tile)
    for row in range(-HALO, ROWS + HALO):
        at = ext_index(row)
        lam = keep(lam_ref[at])
        sibling = from_sibling[at].astype(F32)
        cross = from_cross[at].astype(F32)
        east = jnp.where(even, sibling, cross)
        west = jnp.where(even, cross, sibling)
        east_lam, west_lam = keep(east[0:8]), keep(west[0:8])
        lam_s[at, 0:8] = lam[0:8]
        lam_s[at, 8:16] = jnp.where(sub < 4, lam[8:16], east_lam + pltpu.roll(east_lam, 4, 0))
        lam_s[at, 16:24] = west_lam + pltpu.roll(west_lam, 4, 0)
        for step in range(1, 5):
            reach = HALO - step
            if not -reach <= row < ROWS + reach:
                continue
            place = wind_index(step, row)
            wind = winds_ref[place, :, :lanes].astype(F32)
            ew, ww = east[8:16, :lanes], west[8:16, :lanes]
            if step == 2:
                ew, ww = pltpu.roll(ew, 4, 0), pltpu.roll(ww, 4, 0)
            if step == 3:
                ew, ww = pltpu.roll(ew, 2, 0), pltpu.roll(ww, 6, 0)
            wide_s[place, 0:16] = jnp.concatenate(
                [wind[0:8], jnp.where(sub < 4, wind[8:16], ew)], axis=0
            ).astype(BF16)
            wide_s[place, 16:24] = ww.astype(BF16)


def wind_spread(narrow):
    lanes = 128 if narrow else WIDE
    source = iota((lanes, 2 * lanes), 0)
    lane = iota((lanes, 2 * lanes), 1)
    second = lane >= lanes
    lane = jnp.where(second, lane - lanes, lane)
    if narrow:
        level = jnp.where(lane >= LEVELS, lane - LEVELS, jnp.where(lane >= 16, lane - 16, lane))
        used = level < 8
    else:
        level = lane - jnp.where(lane >= LEVELS, LEVELS, 0) - jnp.where(lane >= 2 * LEVELS, LEVELS, 0)
        used = lane < WIDTH
    match = (source == level + jnp.where(second, LEVELS, 0)) & used
    return jnp.where(match, 0.5, 0.0).astype(BF16)


def advance(lam_a, lam_b, wide_s, coef_s, narrow, emit):
    lat = lax.axis_index("lat")
    has_south = jnp.where(lat > 0, 1.0, 0.0).astype(F32)
    has_north = jnp.where(lat < lax.axis_size("lat") - 1, 1.0, 0.0).astype(F32)
    cols = SUB + 8
    lanes = 128 if narrow else WIDE
    spread = wind_spread(narrow)
    lane = iota((cols, lanes), 1)
    if narrow:
        top = None
        bottom = (lane == 0) | (lane == 16) | (lane == LEVELS)
    else:
        top = (lane == LEVELS - 1) | (lane == 2 * LEVELS - 1) | (lane == 3 * LEVELS - 1)
        bottom = (lane == 0) | (lane == LEVELS) | (lane == 2 * LEVELS)
    now, later = lam_a, lam_b
    for step in range(1, 5):
        reach = HALO - step
        count = ROWS + 2 * reach
        base = wind_index(step, 0)
        lhs = wide_s[base : base + count].reshape(count * cols, lanes)
        coef_s[:count] = jnp.dot(lhs, spread, preferred_element_type=F32).reshape(count, cols, 2 * lanes)
        for row in range(-reach, ROWS + reach):
            at = ext_index(row)
            mid = now[at]
            north = now[ext_index(row + 1)]
            south = now[ext_index(row - 1)]
            east = pltpu.roll(mid, cols - 1, 0)
            west = pltpu.roll(mid, 1, 0)
            upper = pltpu.roll(mid, lanes - 1, 1)
            if top is not None:
                upper = jnp.where(top, mid, upper)
            lower = jnp.where(bottom, mid, pltpu.roll(mid, 1, 1))
            place = wind_index(step, row) - base
            u = coef_s[place, :, :lanes]
            v = coef_s[place, :, lanes:]
            new = (
                CENTER * mid
                + u * (east - west)
                + v * (north - south)
                + HORIZ_MIX * ((east + west) + (north + south))
                + VERT_MIX * (upper + lower)
            )
            if row < 0:
                new = new * has_south
            if row >= ROWS:
                new = new * has_north
            if step < 4:
                later[at] = new
            if 0 <= row < ROWS:
                emit(step, row, new)
        now, later = later, now


def surface_body(
    lam_ref, winds_ref, from_sibling, from_cross, out_ref, lam_a, lam_b, wide_s, coef_s, acc_s
):
    refs = (lam_ref, winds_ref, from_sibling, from_cross)
    assemble(refs, lam_a, wide_s, True)

    def emit(step, row, value):
        acc_s[row] = value[:SUB] if step == 1 else acc_s[row] + value[:SUB]

    advance(lam_a, lam_b, wide_s, coef_s, True, emit)
    lane = iota((SUB, 128), 1)
    surface = jnp.zeros((SUB, 128), F32)
    for row in range(ROWS):
        held = acc_s[row]
        for species, source in enumerate((0, LEVELS, 16)):
            at = row * SPECIES + species
            surface = jnp.where(lane == at, pltpu.roll(held, (at - source) % 128, 1), surface)
    surface = jnp.where(iota((SUB, 128), 0) < ROWS, surface, 0.0)
    block = jnp.where(lane[:8] < 64, surface[0:8], pltpu.roll(surface[8:16], 64, 1))
    both = jnp.concatenate([block, block], axis=0).astype(BF16)
    for pair in range(out_ref.shape[0] // SUB):
        out_ref[SUB * pair : SUB * pair + SUB] = both


def steps_body(lam_ref, winds_ref, from_sibling, from_cross, field_ref, lam_a, lam_b, wide_s, coef_s):
    refs = (lam_ref, winds_ref, from_sibling, from_cross)
    assemble(refs, lam_a, wide_s, False)

    def emit(step, row, value):
        if step == 4:
            field_ref[row] = value[:ROWS, :WIDTH]

    advance(lam_a, lam_b, wide_s, coef_s, False, emit)


def correlation_body(correlation_ref, out_ref):
    total = correlation_ref.shape[1]
    length = total // ROWS * 8
    source = iota((total, length), 0)
    block = iota((total, length), 1) >> 3
    place = iota((total, length), 1) & 7
    first = source == block * ROWS + place
    second = (source == block * ROWS + 8 + place) & (place < 4)
    for index, match in enumerate((first, second)):
        pick = jnp.where(match, 1.0, 0.0).astype(BF16)
        part = jnp.dot(correlation_ref[...], pick, preferred_element_type=F32)
        part = jnp.concatenate([part, jnp.zeros((SUB - ROWS, length), F32)], axis=0)
        out_ref[SUB * index : SUB * index + SUB] = part.astype(BF16)


def gradient_body(surface_ref, correlation_ref, out_ref):
    both = jnp.dot(correlation_ref[...], surface_ref[...], preferred_element_type=F32)
    sums = both[:SUB] + pltpu.roll(both[SUB:], 64, 1)
    result = jnp.transpose(sums)
    for row in range(ROWS):
        out_ref[row] = result[SPECIES * row : SPECIES * row + SPECIES, :ROWS]


def per_device(
    adjoint_in, stored_winds, innovations, columns, kernel_ids, counts, offsets, kernel_table, correlation
):
    lon_count = lax.axis_size("lon")
    lat_count = lax.axis_size("lat")
    shape = jax.ShapeDtypeStruct
    held = innovations.shape[2]
    sent = vmem_call(
        route_body,
        shape((lon_count * CAP, WIDE), BF16),
        [
            pltpu.VMEM((1, lon_count), jnp.int32),
            pltpu.VMEM((1, lon_count), jnp.int32),
            pltpu.VMEM((1, held), jnp.int32),
            pltpu.VMEM((1, held), jnp.int32),
            pltpu.VMEM((WIDTH, held), BF16),
            pltpu.SemaphoreType.DMA((5,)),
        ],
        name="route",
        limit=63 * 1000 * 1000,
        in_specs=[pl.BlockSpec(memory_space=pltpu.HBM)] * 5,
    )(counts, offsets, columns, kernel_ids, jnp.swapaxes(innovations, 2, 3))
    recv = lax.all_to_all(sent, "lon", split_axis=0, concat_axis=0, tiled=True)
    winds = vmem_call(pad_winds_body, shape((4, ROWS, SUB, WIDE), BF16), name="pad_winds")(stored_winds)
    turned = vmem_call(correlation_body, shape((2 * SUB, lon_count * 8), BF16), name="correlation")(correlation.T)
    strip = shape((STRIP, SUB, 128), BF16)
    lam, first, second = vmem_call(
        force_body,
        (shape((ROWS, SUB, WIDE), F32), strip, strip),
        [pltpu.VMEM((3 * kernel_table.shape[0], WIDE), BF16)],
        name="force",
    )(recv, kernel_table, adjoint_in, winds)
    partner = [(i, i ^ 1) for i in range(lat_count) if i ^ 1 < lat_count]
    other = [(i, i + 1 if i % 2 else i - 1) for i in range(1, lat_count - 1 + lat_count % 2)]
    from_first = lax.ppermute(first, "lat", partner)
    from_second = lax.ppermute(second, "lat", other)
    edge = shape((EXT, SUB, WIDE), BF16)
    to_sibling, to_cross, lam_ext, winds_ext = vmem_call(
        edge_body, (edge, edge, shape((EXT, SUB, WIDE), F32), shape((60, SUB, WIDE), BF16)), name="edge"
    )(lam, from_first, from_second, winds)
    from_cross = lax.ppermute(
        to_cross, "lon", [(i, (i + (1 if i % 2 else -1)) % lon_count) for i in range(lon_count)]
    )
    from_sibling = lax.ppermute(to_sibling, "lon", [(i, i ^ 1) for i in range(lon_count)])
    cols = SUB + 8

    def scratch(lanes):
        return [
            pltpu.VMEM((EXT, cols, lanes), F32),
            pltpu.VMEM((EXT, cols, lanes), F32),
            pltpu.VMEM((60, cols, lanes), BF16),
            pltpu.VMEM((EXT, cols, 2 * lanes), F32),
        ]

    state = (lam_ext, winds_ext, from_sibling, from_cross)
    surface = vmem_call(
        surface_body,
        shape((lon_count * 8, 128), BF16),
        scratch(128) + [pltpu.VMEM((ROWS, SUB, 128), F32)],
        name="surface",
    )(*state)
    gathered = lax.all_to_all(surface, "lon", split_axis=0, concat_axis=0, tiled=True)
    field = vmem_call(steps_body, shape((ROWS, ROWS, WIDTH), F32), scratch(WIDE), name="steps")(*state)
    gradient = vmem_call(gradient_body, shape((ROWS, SPECIES, ROWS), F32), name="gradient")(gathered, turned)
    return field, gradient


def solution(mesh):
    return jax.shard_map(
        per_device,
        mesh=mesh,
        in_specs=(
            P("lat", "lon", None),
            P(None, "lat", "lon", None),
            P("lat", "lon", None, None),
            P("lat", "lon", None),
            P("lat", "lon", None),
            P("lat", "lon", None),
            P("lat", "lon", None),
            P(),
            P(None, "lon"),
        ),
        out_specs=(P("lat", "lon", None), P("lat", None, "lon")),
        check_vma=False,
    )
```

```python
import functools

import jax
import jax.numpy as jnp
from jax import lax
from jax.experimental import pallas as pl
from jax.experimental.pallas import tpu as pltpu
from jax.sharding import PartitionSpec as P

CAP = 8
HORIZ_MIX = 0.18
VERT_MIX = 0.1
CENTER = 1.0 - 4.0 * HORIZ_MIX - 2.0 * VERT_MIX

ROWS = 12
HALO = 4
SUB = 16
WIDE = 256
LEVELS = 72
SPECIES = 3
WIDTH = SPECIES * LEVELS
CODE_LANE = 216
KERNEL_LANE = 217
F32 = jnp.float32
BF16 = jnp.bfloat16


def iota(shape, dim):
    return lax.broadcasted_iota(jnp.int32, shape, dim)


def vmem_call(body, outs, scratch=(), name=None, limit=48 * 1024 * 1024, **specs):
    return pl.pallas_call(
        body,
        out_shape=outs,
        scratch_shapes=list(scratch),
        name=name,
        compiler_params=pltpu.CompilerParams(vmem_limit_bytes=limit),
        **specs,
    )


def route_body(
    counts_hbm, offsets_hbm, columns_hbm, kernels_hbm, innov_hbm, out_ref,
    counts_s, offsets_s, columns_s, kernels_s, innov_s, sems,
):
    moves = (
        (counts_hbm.at[0], counts_s),
        (offsets_hbm.at[0], offsets_s),
        (columns_hbm.at[0], columns_s),
        (kernels_hbm.at[0], kernels_s),
        (innov_hbm.at[0, 0], innov_s),
    )
    copies = [pltpu.make_async_copy(source, target, sems.at[i]) for i, (source, target) in enumerate(moves)]
    for copy in copies:
        copy.start()
    for copy in copies[:4]:
        copy.wait()
    held = innov_s.shape[1]
    owners = counts_s.shape[1]
    eye = iota((owners, owners), 0) == iota((owners, owners), 1)
    offset_col = jnp.sum(jnp.where(eye, offsets_s[...].astype(F32), 0.0), axis=1, keepdims=True)
    count_col = jnp.sum(jnp.where(eye, counts_s[...].astype(F32), 0.0), axis=1, keepdims=True)
    place = iota((owners, held), 1).astype(F32) - offset_col
    place = jnp.where(place < count_col, place, -1.0)
    slot = iota((owners, CAP, held), 1).astype(F32)
    pick = jnp.where(place[:, None, :] == slot, 1.0, 0.0).reshape(owners * CAP, held).astype(BF16)
    cell = columns_s[...]
    code = (cell + 4 * ((cell * 171) >> 11) + 1).astype(F32)
    half = WIDE // 2
    line = iota((half, held), 0)
    codes = jnp.where(
        line == CODE_LANE - half,
        code,
        jnp.where(line == KERNEL_LANE - half, kernels_s[...].astype(F32), 0.0),
    ).astype(BF16)
    tail = lax.dot_general(pick, codes, (((1,), (1,)), ((), ())), preferred_element_type=F32)
    out_ref[:, half:] = tail.astype(BF16)
    copies[4].wait()
    sent = lax.dot_general(
        pick, innov_s[...], (((1,), (1,)), ((), ())), preferred_element_type=F32
    ).astype(BF16)
    out_ref[:, :half] = sent[:, :half]
    out_ref[:, half:WIDTH] = sent[:, half:]


def pad_winds_body(winds_ref, out_ref):
    out_ref[...] = jnp.zeros_like(out_ref)
    out_ref[:, :, :ROWS, : 2 * LEVELS] = winds_ref[...]


STRIP = 11
SPARE = (WIDTH - 128, WIDTH - 112)


def pieces(row):
    return pltpu.roll(row[0:8], 4, 0), row[0:8], pltpu.roll(row[8:16], 4, 0)


def with_piece(row, piece):
    sub = iota((8, row.shape[1]), 0)
    return jnp.concatenate([row[0:8], jnp.where(sub < 4, row[8:16], piece)], axis=0)


def pack_strip(lam_rows, wind_rows):
    extra = pieces(lam_rows[3])
    lane = iota((SUB, 128), 1)
    halves = []
    for index in range(3):
        packed = with_piece(lam_rows[index], extra[index])
        one, two = (pltpu.roll(wind_rows[index + 3 * i][:, 128:], SPARE[i], 1) for i in range(2))
        halves += [
            packed[:, :128],
            jnp.where(lane < SPARE[0], packed[:, 128:], jnp.where(lane < SPARE[1], one, two)),
        ]
    main = [row[:, :128] for row in wind_rows]
    extra = pieces(main[4])
    halves += [with_piece(main[index], extra[index]) for index in range(3)] + [main[3], main[5]]
    return halves


def rejoin(tiles):
    first, second, third = (tile[8:16] for tile in tiles)
    sub = iota(first.shape, 0)
    return jnp.concatenate([jnp.where(sub < 4, pltpu.roll(first, 4, 0), second), pltpu.roll(third, 4, 0)], axis=0)


def unpack_strip(halves):
    tiles = [jnp.concatenate(halves[2 * i : 2 * i + 2], axis=1) for i in range(3)]
    lam_rows = tiles + [rejoin(tiles)]
    main = halves[6:10] + [rejoin(halves[6:9]), halves[10]]
    wind_rows = []
    for index in range(6):
        last = pltpu.roll(halves[2 * (index % 3) + 1], 128 - SPARE[index // 3], 1)
        wind_rows.append(jnp.concatenate([main[index], last], axis=1))
    return lam_rows, wind_rows


def force_body(recv_ref, table_ref, adjoint_ref, winds_ref, lam_ref, north_ref, south_ref, table_s):
    total = recv_ref.shape[0]
    nkernel = table_ref.shape[0]
    recv = recv_ref[...]
    wide = recv.astype(F32)
    pick = jnp.where((iota((8, WIDE), 1) == CODE_LANE), 1.0, 0.0).astype(BF16)
    code_line = lax.dot_general(pick, recv, (((1,), (1,)), ((), ())), preferred_element_type=F32)
    kernel_col = wide[:, KERNEL_LANE : KERNEL_LANE + 1]
    lane = iota((total, 3 * nkernel), 1)
    lane = (lane - jnp.where(lane >= nkernel, nkernel, 0) - jnp.where(lane >= 2 * nkernel, nkernel, 0)).astype(F32)
    onehot = jnp.where(kernel_col == lane, 1.0, 0.0).astype(BF16)
    table = table_ref[...]
    table_s[...] = jnp.zeros_like(table_s)
    high = table.astype(BF16)
    rest = table - high.astype(F32)
    middle = rest.astype(BF16)
    table_s[0:nkernel, :WIDTH] = high
    table_s[nkernel : 2 * nkernel, :WIDTH] = middle
    table_s[2 * nkernel :, :WIDTH] = (rest - middle.astype(F32)).astype(BF16)
    weights = jnp.dot(onehot, table_s[...], preferred_element_type=F32)
    weighted = wide * weights
    whigh = weighted.astype(BF16)
    wlow = (weighted - whigh.astype(F32)).astype(BF16)
    cell = (iota((ROWS * SUB, total), 0) + 1).astype(F32)
    scatter = jnp.where(cell == code_line[0:1, :], 1.0, 0.0).astype(BF16)
    force = jnp.dot(scatter, whigh, preferred_element_type=F32) + jnp.dot(
        scatter, wlow, preferred_element_type=F32
    )
    lam_ref[...] = force.reshape(ROWS, SUB, WIDE)
    lam_ref[:, :ROWS, :WIDTH] = lam_ref[:, :ROWS, :WIDTH] + adjoint_ref[...]
    for lower, strip in ((False, north_ref), (True, south_ref)):
        start = 0 if lower else ROWS - HALO
        wind_rows = []
        for step in (1, 2, 3):
            depth = HALO - step
            begin = 0 if lower else ROWS - depth
            wind_rows += [winds_ref[4 - step, begin + i].astype(F32) for i in range(depth)]
        for index, half in enumerate(pack_strip([lam_ref[start + i] for i in range(HALO)], wind_rows)):
            strip[index] = half.astype(BF16)


WIND_FIRST = {1: 0, 2: 3, 3: 5}
EXT = ROWS + 2 * HALO


def ext_index(row):
    return row if row >= 0 else row + EXT


def wind_index(step, row):
    base = (0, 18, 34, 48)[step - 1]
    reach = HALO - step
    return base + (row if row >= 0 else row + ROWS + 2 * reach)


def edge_body(lam_ref, from_south, from_north, winds_ref, sibling_ref, cross_ref, lam_out, winds_out):
    south_lam, south_winds = unpack_strip([from_south[i].astype(F32) for i in range(STRIP)])
    north_lam, north_winds = unpack_strip([from_north[i].astype(F32) for i in range(STRIP)])
    even = lax.rem(lax.axis_index("lon"), 2) == 0
    sub = iota((8, WIDE), 0)
    lane = iota((8, 128), 1)
    none = jnp.zeros((SUB, WIDE), F32)
    held = {}
    for row in sorted(range(-HALO, ROWS + HALO), key=ext_index):
        own = 0 <= row < ROWS
        lam = lam_ref[row] if own else (south_lam[row + HALO] if row < 0 else north_lam[row - ROWS])
        lam_out[ext_index(row)] = lam
        wind = {}
        for step in (1, 2, 3, 4):
            reach = HALO - step
            if own:
                raw = winds_ref[4 - step, row]
                winds_out[wind_index(step, row)] = raw
                wind[step] = raw.astype(F32)
            elif -reach <= row < ROWS + reach:
                rows, at = (south_winds, row + reach) if row < 0 else (north_winds, row - ROWS)
                wind[step] = rows[WIND_FIRST[step] + at]
                winds_out[wind_index(step, row)] = wind[step].astype(BF16)
            else:
                wind[step] = none
        made = []
        for tile in (1, 0):
            cut = slice(8 * tile, 8 * tile + 8)
            upper = pltpu.roll(wind[1][cut], 4, 0)
            if tile == 1:
                rest = jnp.where(sub >= 2, wind[2][cut], pltpu.roll(wind[3][cut], 6, 0))
            else:
                rest = jnp.where(sub < 2, wind[2][cut], pltpu.roll(wind[3][cut], 2, 0))
            made.append((lam[cut], jnp.where(sub >= 4, upper, rest)))
        if ext_index(row) % 2 == 0:
            held = made
            continue
        strips = []
        for (lam_a, wind_a), (lam_b, wind_b) in zip(held, made, strict=True):
            both = jnp.where(sub < 4, lam_a, pltpu.roll(lam_b, 4, 0))
            one = pltpu.roll(wind_a[:, 128:], SPARE[0], 1)
            two = pltpu.roll(wind_b[:, 128:], SPARE[1], 1)
            last = jnp.where(lane < SPARE[0], both[:, 128:], jnp.where(lane < SPARE[1], one, two))
            upper = jnp.concatenate([both[:, :128], last], axis=1)
            lower = jnp.concatenate([wind_a[:, :128], wind_b[:, :128]], axis=1)
            strips.append(jnp.concatenate([upper, lower], axis=0))
        to_east, to_west = strips
        sibling_ref[ext_index(row) // 2] = jnp.where(even, to_east, to_west).astype(BF16)
        cross_ref[ext_index(row) // 2] = jnp.where(even, to_west, to_east).astype(BF16)


def pack_low(tile):
    lane = iota(tile.shape[:-1] + (128,), len(tile.shape) - 1)
    return jnp.where((lane >= 16) & (lane < 24), tile[..., 128:], tile[..., :128])


def assemble(refs, lam_s, wide_s, narrow):
    lam_ref, winds_ref, from_cross, from_sibling = refs
    even = lax.rem(lax.axis_index("lon"), 2) == 0
    sub = iota((8, 128 if narrow else WIDE), 0)
    lanes = 128 if narrow else WIDE
    keep = pack_low if narrow else (lambda tile: tile)
    for row in range(-HALO, ROWS + HALO):
        at = ext_index(row)
        lam = keep(lam_ref[at])
        sibling = from_sibling[at // 2].astype(F32)
        cross = from_cross[at // 2].astype(F32)
        east = jnp.where(even, sibling, cross)
        west = jnp.where(even, cross, sibling)
        odd = at % 2
        east_lam, west_lam = keep(east[0:8]), keep(west[0:8])
        if not odd:
            east_lam, west_lam = pltpu.roll(east_lam, 4, 0), pltpu.roll(west_lam, 4, 0)
        lam_s[at, 0:8] = lam[0:8]
        lam_s[at, 8:16] = jnp.where(sub < 4, lam[8:16], east_lam)
        lam_s[at, 16:24] = west_lam
        east_wind, west_wind = (side[8:16, 128 * odd : 128 * odd + 128] for side in (east, west))
        if not narrow:
            east_wind, west_wind = (
                jnp.concatenate([main, pltpu.roll(side[0:8, 128:], 128 - SPARE[odd], 1)], axis=1)
                for main, side in ((east_wind, east), (west_wind, west))
            )
        for step in range(1, 5):
            reach = HALO - step
            if not -reach <= row < ROWS + reach:
                continue
            place = wind_index(step, row)
            wind = winds_ref[place, :, :lanes].astype(F32)
            ew, ww = east_wind, west_wind
            if step == 2:
                ew, ww = pltpu.roll(ew, 4, 0), pltpu.roll(ww, 4, 0)
            if step == 3:
                ew, ww = pltpu.roll(ew, 2, 0), pltpu.roll(ww, 6, 0)
            wide_s[place, 0:16] = jnp.concatenate(
                [wind[0:8], jnp.where(sub < 4, wind[8:16], ew)], axis=0
            ).astype(BF16)
            wide_s[place, 16:24] = ww.astype(BF16)


def wind_spread(narrow):
    lanes = 128 if narrow else WIDE
    source = iota((lanes, 2 * lanes), 0)
    lane = iota((lanes, 2 * lanes), 1)
    second = lane >= lanes
    lane = jnp.where(second, lane - lanes, lane)
    if narrow:
        level = jnp.where(lane >= LEVELS, lane - LEVELS, jnp.where(lane >= 16, lane - 16, lane))
        used = level < 8
    else:
        level = lane - jnp.where(lane >= LEVELS, LEVELS, 0) - jnp.where(lane >= 2 * LEVELS, LEVELS, 0)
        used = lane < WIDTH
    match = (source == level + jnp.where(second, LEVELS, 0)) & used
    return jnp.where(match, 0.5, 0.0).astype(BF16)


def advance(lam_a, lam_b, wide_s, coef_s, narrow, emit):
    lat = lax.axis_index("lat")
    has_south = jnp.where(lat > 0, 1.0, 0.0).astype(F32)
    has_north = jnp.where(lat < lax.axis_size("lat") - 1, 1.0, 0.0).astype(F32)
    cols = SUB + 8
    lanes = 128 if narrow else WIDE
    spread = wind_spread(narrow)
    lane = iota((cols, lanes), 1)
    if narrow:
        top = None
        bottom = (lane == 0) | (lane == 16) | (lane == LEVELS)
    else:
        top = (lane == LEVELS - 1) | (lane == 2 * LEVELS - 1) | (lane == 3 * LEVELS - 1)
        bottom = (lane == 0) | (lane == LEVELS) | (lane == 2 * LEVELS)
    now, later = lam_a, lam_b
    for step in range(1, 5):
        reach = HALO - step
        count = ROWS + 2 * reach
        base = wind_index(step, 0)
        lhs = wide_s[base : base + count].reshape(count * cols, lanes)
        coef_s[:count] = jnp.dot(lhs, spread, preferred_element_type=F32).reshape(count, cols, 2 * lanes)
        for row in range(-reach, ROWS + reach):
            at = ext_index(row)
            mid = now[at]
            north = now[ext_index(row + 1)]
            south = now[ext_index(row - 1)]
            east = pltpu.roll(mid, cols - 1, 0)
            west = pltpu.roll(mid, 1, 0)
            upper = pltpu.roll(mid, lanes - 1, 1)
            if top is not None:
                upper = jnp.where(top, mid, upper)
            lower = jnp.where(bottom, mid, pltpu.roll(mid, 1, 1))
            place = wind_index(step, row) - base
            u = coef_s[place, :, :lanes]
            v = coef_s[place, :, lanes:]
            new = (
                CENTER * mid
                + u * (east - west)
                + v * (north - south)
                + HORIZ_MIX * ((east + west) + (north + south))
                + VERT_MIX * (upper + lower)
            )
            if row < 0:
                new = new * has_south
            if row >= ROWS:
                new = new * has_north
            if step < 4:
                later[at] = new
            if 0 <= row < ROWS:
                emit(step, row, new)
        now, later = later, now


def surface_body(
    lam_ref, winds_ref, from_cross, from_sibling, out_ref, lam_a, lam_b, wide_s, coef_s, acc_s
):
    refs = (lam_ref, winds_ref, from_cross, from_sibling)
    assemble(refs, lam_a, wide_s, True)

    def emit(step, row, value):
        acc_s[row] = value[:SUB] if step == 1 else acc_s[row] + value[:SUB]

    advance(lam_a, lam_b, wide_s, coef_s, True, emit)
    lane = iota((SUB, 128), 1)
    surface = jnp.zeros((SUB, 128), F32)
    for row in range(ROWS):
        held = acc_s[row]
        for species, source in enumerate((0, LEVELS, 16)):
            at = row * SPECIES + species
            surface = jnp.where(lane == at, pltpu.roll(held, (at - source) % 128, 1), surface)
    surface = jnp.where(iota((SUB, 128), 0) < ROWS, surface, 0.0)
    block = jnp.where(lane[:8] < 64, surface[0:8], pltpu.roll(surface[8:16], 64, 1))
    both = jnp.concatenate([block, block], axis=0).astype(BF16)
    for pair in range(out_ref.shape[0] // SUB):
        out_ref[SUB * pair : SUB * pair + SUB] = both


def steps_body(lam_ref, winds_ref, from_cross, from_sibling, field_ref, lam_a, lam_b, wide_s, coef_s):
    refs = (lam_ref, winds_ref, from_cross, from_sibling)
    assemble(refs, lam_a, wide_s, False)

    def emit(step, row, value):
        if step == 4:
            field_ref[row] = value[:ROWS, :WIDTH]

    advance(lam_a, lam_b, wide_s, coef_s, False, emit)


def correlation_body(correlation_ref, out_ref):
    total = correlation_ref.shape[1]
    length = total // ROWS * 8
    source = iota((total, length), 0)
    block = iota((total, length), 1) >> 3
    place = iota((total, length), 1) & 7
    first = source == block * ROWS + place
    second = (source == block * ROWS + 8 + place) & (place < 4)
    for index, match in enumerate((first, second)):
        pick = jnp.where(match, 1.0, 0.0).astype(BF16)
        part = jnp.dot(correlation_ref[...], pick, preferred_element_type=F32)
        part = jnp.concatenate([part, jnp.zeros((SUB - ROWS, length), F32)], axis=0)
        out_ref[SUB * index : SUB * index + SUB] = part.astype(BF16)


def gradient_body(surface_ref, correlation_ref, out_ref):
    both = jnp.dot(correlation_ref[...], surface_ref[...], preferred_element_type=F32)
    sums = both[:SUB] + pltpu.roll(both[SUB:], 64, 1)
    result = jnp.transpose(sums)
    for row in range(ROWS):
        out_ref[row] = result[SPECIES * row : SPECIES * row + SPECIES, :ROWS]


def per_device(
    adjoint_in, stored_winds, innovations, columns, kernel_ids, counts, offsets, kernel_table, correlation
):
    lon_count = lax.axis_size("lon")
    lat_count = lax.axis_size("lat")
    shape = jax.ShapeDtypeStruct
    held = innovations.shape[2]
    sent = vmem_call(
        route_body,
        shape((lon_count * CAP, WIDE), BF16),
        [
            pltpu.VMEM((1, lon_count), jnp.int32),
            pltpu.VMEM((1, lon_count), jnp.int32),
            pltpu.VMEM((1, held), jnp.int32),
            pltpu.VMEM((1, held), jnp.int32),
            pltpu.VMEM((WIDTH, held), BF16),
            pltpu.SemaphoreType.DMA((5,)),
        ],
        name="route",
        limit=63 * 1000 * 1000,
        in_specs=[pl.BlockSpec(memory_space=pltpu.HBM)] * 5,
    )(counts, offsets, columns, kernel_ids, jnp.swapaxes(innovations, 2, 3))
    recv = lax.all_to_all(sent, "lon", split_axis=0, concat_axis=0, tiled=True)
    winds = vmem_call(pad_winds_body, shape((4, ROWS, SUB, WIDE), BF16), name="pad_winds")(stored_winds)
    turned = vmem_call(correlation_body, shape((2 * SUB, lon_count * 8), BF16), name="correlation")(correlation.T)
    strip = shape((STRIP, SUB, 128), BF16)
    lam, north, south = vmem_call(
        force_body,
        (shape((ROWS, SUB, WIDE), F32), strip, strip),
        [pltpu.VMEM((3 * kernel_table.shape[0], WIDE), BF16)],
        name="force",
    )(recv, kernel_table, adjoint_in, winds)
    up = [(i, i + 1) for i in range(lat_count - 1)]
    down = [(i + 1, i) for i in range(lat_count - 1)]
    from_south = lax.ppermute(north, "lat", up)
    from_north = lax.ppermute(south, "lat", down)
    edge = shape((EXT // 2, SUB, WIDE), BF16)
    to_sibling, to_cross, lam_ext, winds_ext = vmem_call(
        edge_body, (edge, edge, shape((EXT, SUB, WIDE), F32), shape((60, SUB, WIDE), BF16)), name="edge"
    )(lam, from_south, from_north, winds)
    from_cross = lax.ppermute(
        to_cross, "lon", [(i, (i + (1 if i % 2 else -1)) % lon_count) for i in range(lon_count)]
    )
    from_sibling = lax.ppermute(to_sibling, "lon", [(i, i ^ 1) for i in range(lon_count)])
    cols = SUB + 8

    def scratch(lanes):
        return [
            pltpu.VMEM((EXT, cols, lanes), F32),
            pltpu.VMEM((EXT, cols, lanes), F32),
            pltpu.VMEM((60, cols, lanes), BF16),
            pltpu.VMEM((EXT, cols, 2 * lanes), F32),
        ]

    state = (lam_ext, winds_ext, from_cross, from_sibling)
    surface = vmem_call(
        surface_body,
        shape((lon_count * 8, 128), BF16),
        scratch(128) + [pltpu.VMEM((ROWS, SUB, 128), F32)],
        name="surface",
    )(*state)
    gathered = lax.all_to_all(surface, "lon", split_axis=0, concat_axis=0, tiled=True)
    field = vmem_call(steps_body, shape((ROWS, ROWS, WIDTH), F32), scratch(WIDE), name="steps")(*state)
    gradient = vmem_call(gradient_body, shape((ROWS, SPECIES, ROWS), F32), name="gradient")(gathered, turned)
    return field, gradient


def solution(mesh):
    return jax.shard_map(
        per_device,
        mesh=mesh,
        in_specs=(
            P("lat", "lon", None),
            P(None, "lat", "lon", None),
            P("lat", "lon", None, None),
            P("lat", "lon", None),
            P("lat", "lon", None),
            P("lat", "lon", None),
            P("lat", "lon", None),
            P(),
            P(None, "lon"),
        ),
        out_specs=(P("lat", "lon", None), P("lat", None, "lon")),
        check_vma=False,
    )
```

```python
import functools

import jax
import jax.numpy as jnp
from jax import lax
from jax.experimental import pallas as pl
from jax.experimental.pallas import tpu as pltpu
from jax.sharding import PartitionSpec as P

CAP = 8
HORIZ_MIX = 0.18
VERT_MIX = 0.1
CENTER = 1.0 - 4.0 * HORIZ_MIX - 2.0 * VERT_MIX

ROWS = 12
HALO = 4
SUB = 16
WIDE = 256
LEVELS = 72
SPECIES = 3
WIDTH = SPECIES * LEVELS
CODE_LANE = 216
KERNEL_LANE = 217
F32 = jnp.float32
BF16 = jnp.bfloat16


def iota(shape, dim):
    return lax.broadcasted_iota(jnp.int32, shape, dim)


def vmem_call(body, outs, scratch=(), name=None, limit=48 * 1024 * 1024, **specs):
    return pl.pallas_call(
        body,
        out_shape=outs,
        scratch_shapes=list(scratch),
        name=name,
        compiler_params=pltpu.CompilerParams(vmem_limit_bytes=limit),
        **specs,
    )


def route_body(
    counts_hbm, offsets_hbm, columns_hbm, kernels_hbm, innov_hbm, out_ref,
    counts_s, offsets_s, columns_s, kernels_s, innov_s, sems,
):
    moves = (
        (counts_hbm.at[0], counts_s),
        (offsets_hbm.at[0], offsets_s),
        (columns_hbm.at[0], columns_s),
        (kernels_hbm.at[0], kernels_s),
        (innov_hbm.at[0, 0], innov_s),
    )
    copies = [pltpu.make_async_copy(source, target, sems.at[i]) for i, (source, target) in enumerate(moves)]
    for copy in copies:
        copy.start()
    for copy in copies[:4]:
        copy.wait()
    held = innov_s.shape[1]
    owners = counts_s.shape[1]
    eye = iota((owners, owners), 0) == iota((owners, owners), 1)
    offset_col = jnp.sum(jnp.where(eye, offsets_s[...].astype(F32), 0.0), axis=1, keepdims=True)
    count_col = jnp.sum(jnp.where(eye, counts_s[...].astype(F32), 0.0), axis=1, keepdims=True)
    place = iota((owners, held), 1).astype(F32) - offset_col
    place = jnp.where(place < count_col, place, -1.0)
    slot = iota((owners, CAP, held), 1).astype(F32)
    pick = jnp.where(place[:, None, :] == slot, 1.0, 0.0).reshape(owners * CAP, held).astype(BF16)
    cell = columns_s[...]
    code = (cell + 4 * ((cell * 171) >> 11) + 1).astype(F32)
    half = WIDE // 2
    line = iota((half, held), 0)
    codes = jnp.where(
        line == CODE_LANE - half,
        code,
        jnp.where(line == KERNEL_LANE - half, kernels_s[...].astype(F32), 0.0),
    ).astype(BF16)
    tail = lax.dot_general(pick, codes, (((1,), (1,)), ((), ())), preferred_element_type=F32)
    out_ref[:, half:] = tail.astype(BF16)
    copies[4].wait()
    sent = lax.dot_general(
        pick, innov_s[...], (((1,), (1,)), ((), ())), preferred_element_type=F32
    ).astype(BF16)
    out_ref[:, :half] = sent[:, :half]
    out_ref[:, half:WIDTH] = sent[:, half:]


def pack_levels(tiles):
    lane = iota(tiles[0].shape, 1)
    lane = jnp.where(lane >= LEVELS, lane - LEVELS, lane)
    packed = tiles[0]
    for index in range(1, len(tiles)):
        packed = jnp.where(lane >= 4 * index, pltpu.roll(tiles[index], 4 * index, 1), packed)
    return packed


def winds_body(winds_ref, out_ref, sibling_ref, cross_ref):
    out_ref[...] = jnp.zeros_like(out_ref)
    out_ref[:, :, :ROWS, : 2 * LEVELS] = winds_ref[...]
    even = lax.rem(lax.axis_index("lon"), 2) == 0
    sub = iota((8, 128), 0)
    made = []
    for tile in (1, 0):
        rows = []
        for row in range(ROWS):
            cuts = [out_ref[4 - step, row, :, :128].astype(F32)[8 * tile : 8 * tile + 8] for step in (1, 2, 3, 4)]
            parts = [jnp.where(sub < 4, cuts[i], pltpu.roll(cuts[i + 1], 4, 0)) for i in (0, 2)]
            rows.append(jnp.concatenate(parts, axis=0))
        made.append(pack_levels(rows))
    to_east, to_west = made
    sibling_ref[...] = jnp.where(even, to_east, to_west).astype(BF16)
    cross_ref[...] = jnp.where(even, to_west, to_east).astype(BF16)


def edge_winds(from_cross, from_sibling, row):
    even = lax.rem(lax.axis_index("lon"), 2) == 0
    sibling = from_sibling[...].astype(F32)
    cross = from_cross[...].astype(F32)
    sides = []
    for side in (jnp.where(even, sibling, cross), jnp.where(even, cross, sibling)):
        if row:
            side = pltpu.roll(side, 128 - 4 * row, 1)
        first, second = side[0:8], side[8:16]
        sides.append({1: pltpu.roll(first, 4, 0), 2: first, 3: pltpu.roll(second, 4, 0), 4: second})
    return sides


STRIP = 11
SPARE = (WIDTH - 128, WIDTH - 112)


def pieces(row):
    return pltpu.roll(row[0:8], 4, 0), row[0:8], pltpu.roll(row[8:16], 4, 0)


def with_piece(row, piece):
    sub = iota((8, row.shape[1]), 0)
    return jnp.concatenate([row[0:8], jnp.where(sub < 4, row[8:16], piece)], axis=0)


def pack_strip(lam_rows, wind_rows, east, west):
    extra = pieces(lam_rows[3])
    lane = iota((SUB, 128), 1)
    halves = []
    for index in range(3):
        packed = with_piece(lam_rows[index], extra[index])
        one, two = (pltpu.roll(wind_rows[index + 3 * i][:, 128:], SPARE[i], 1) for i in range(2))
        halves += [
            packed[:, :128],
            jnp.where(lane < SPARE[0], packed[:, 128:], jnp.where(lane < SPARE[1], one, two)),
        ]
    main = [row[:, :128] for row in wind_rows]
    extra = pieces(main[4])
    halves += [with_piece(main[index], extra[index]) for index in range(3)]
    halves += [with_piece(main[3], pack_levels(east)), with_piece(main[5], pack_levels(west))]
    return halves


def rejoin(tiles):
    first, second, third = (tile[8:16] for tile in tiles)
    sub = iota(first.shape, 0)
    return jnp.concatenate([jnp.where(sub < 4, pltpu.roll(first, 4, 0), second), pltpu.roll(third, 4, 0)], axis=0)


def unpack_strip(halves):
    tiles = [jnp.concatenate(halves[2 * i : 2 * i + 2], axis=1) for i in range(3)]
    lam_rows = tiles + [rejoin(tiles)]
    main = halves[6:10] + [rejoin(halves[6:9]), halves[10]]
    wind_rows = []
    for index in range(6):
        last = pltpu.roll(halves[2 * (index % 3) + 1], 128 - SPARE[index // 3], 1)
        wind_rows.append(jnp.concatenate([main[index], last], axis=1))
    return lam_rows, wind_rows


def force_body(
    recv_ref, table_ref, adjoint_ref, winds_ref, from_cross, from_sibling, lam_ref, north_ref, south_ref, table_s
):
    total = recv_ref.shape[0]
    nkernel = table_ref.shape[0]
    recv = recv_ref[...]
    wide = recv.astype(F32)
    pick = jnp.where((iota((8, WIDE), 1) == CODE_LANE), 1.0, 0.0).astype(BF16)
    code_line = lax.dot_general(pick, recv, (((1,), (1,)), ((), ())), preferred_element_type=F32)
    kernel_col = wide[:, KERNEL_LANE : KERNEL_LANE + 1]
    lane = iota((total, 3 * nkernel), 1)
    lane = (lane - jnp.where(lane >= nkernel, nkernel, 0) - jnp.where(lane >= 2 * nkernel, nkernel, 0)).astype(F32)
    onehot = jnp.where(kernel_col == lane, 1.0, 0.0).astype(BF16)
    table = table_ref[...]
    table_s[...] = jnp.zeros_like(table_s)
    high = table.astype(BF16)
    rest = table - high.astype(F32)
    middle = rest.astype(BF16)
    table_s[0:nkernel, :WIDTH] = high
    table_s[nkernel : 2 * nkernel, :WIDTH] = middle
    table_s[2 * nkernel :, :WIDTH] = (rest - middle.astype(F32)).astype(BF16)
    weights = jnp.dot(onehot, table_s[...], preferred_element_type=F32)
    weighted = wide * weights
    whigh = weighted.astype(BF16)
    wlow = (weighted - whigh.astype(F32)).astype(BF16)
    cell = (iota((ROWS * SUB, total), 0) + 1).astype(F32)
    scatter = jnp.where(cell == code_line[0:1, :], 1.0, 0.0).astype(BF16)
    force = jnp.dot(scatter, whigh, preferred_element_type=F32) + jnp.dot(
        scatter, wlow, preferred_element_type=F32
    )
    lam_ref[...] = force.reshape(ROWS, SUB, WIDE)
    lam_ref[:, :ROWS, :WIDTH] = lam_ref[:, :ROWS, :WIDTH] + adjoint_ref[...]
    for lower, strip in ((False, north_ref), (True, south_ref)):
        start = 0 if lower else ROWS - HALO
        wind_rows, east, west = [], [], []
        for step in (1, 2, 3):
            depth = HALO - step
            begin = 0 if lower else ROWS - depth
            for row in range(begin, begin + depth):
                wind_rows.append(winds_ref[4 - step, row].astype(F32))
                sides = edge_winds(from_cross, from_sibling, row)
                east.append(sides[0][step])
                west.append(sides[1][step])
        for index, half in enumerate(pack_strip([lam_ref[start + i] for i in range(HALO)], wind_rows, east, west)):
            strip[index] = half.astype(BF16)


WIND_FIRST = {1: 0, 2: 3, 3: 5}
EXT = ROWS + 2 * HALO


def ext_index(row):
    return row if row >= 0 else row + EXT


def wind_index(step, row):
    base = (0, 18, 34, 48)[step - 1]
    reach = HALO - step
    return base + (row if row >= 0 else row + ROWS + 2 * reach)


def edge_body(lam_ref, from_south, from_north, winds_ref, _, sibling_ref, cross_ref, lam_out, winds_out):
    south_lam, south_winds = unpack_strip([from_south[i].astype(F32) for i in range(STRIP)])
    north_lam, north_winds = unpack_strip([from_north[i].astype(F32) for i in range(STRIP)])
    even = lax.rem(lax.axis_index("lon"), 2) == 0
    sub = iota((8, WIDE), 0)
    lane = iota((8, 128), 1)
    none = jnp.zeros((SUB, WIDE), F32)
    held = {}
    for row in sorted(range(-HALO, ROWS + HALO), key=ext_index):
        own = 0 <= row < ROWS
        lam = lam_ref[row] if own else (south_lam[row + HALO] if row < 0 else north_lam[row - ROWS])
        lam_out[ext_index(row)] = lam
        wind = {}
        for step in (1, 2, 3, 4):
            reach = HALO - step
            if own:
                raw = winds_ref[4 - step, row]
                winds_out[wind_index(step, row)] = raw
                wind[step] = raw.astype(F32)
            elif -reach <= row < ROWS + reach:
                rows, at = (south_winds, row + reach) if row < 0 else (north_winds, row - ROWS)
                wind[step] = rows[WIND_FIRST[step] + at]
                winds_out[wind_index(step, row)] = wind[step].astype(BF16)
            else:
                wind[step] = none
        made = []
        for tile in (1, 0):
            cut = slice(8 * tile, 8 * tile + 8)
            upper = pltpu.roll(wind[1][cut], 4, 0)
            if tile == 1:
                rest = jnp.where(sub >= 2, wind[2][cut], pltpu.roll(wind[3][cut], 6, 0))
            else:
                rest = jnp.where(sub < 2, wind[2][cut], pltpu.roll(wind[3][cut], 2, 0))
            made.append((lam[cut], jnp.where(sub >= 4, upper, rest)))
        if ext_index(row) % 2 == 0:
            held = made
            continue
        strips = []
        for (lam_a, wind_a), (lam_b, wind_b) in zip(held, made, strict=True):
            both = jnp.where(sub < 4, lam_a, pltpu.roll(lam_b, 4, 0))
            one = pltpu.roll(wind_a[:, 128:], SPARE[0], 1)
            two = pltpu.roll(wind_b[:, 128:], SPARE[1], 1)
            last = jnp.where(lane < SPARE[0], both[:, 128:], jnp.where(lane < SPARE[1], one, two))
            upper = jnp.concatenate([both[:, :128], last], axis=1)
            lower = jnp.concatenate([wind_a[:, :128], wind_b[:, :128]], axis=1)
            strips.append(jnp.concatenate([upper, lower], axis=0))
        to_east, to_west = strips
        sibling_ref[ext_index(row) // 2] = jnp.where(even, to_east, to_west).astype(BF16)
        cross_ref[ext_index(row) // 2] = jnp.where(even, to_west, to_east).astype(BF16)


def pack_low(tile):
    lane = iota(tile.shape[:-1] + (128,), len(tile.shape) - 1)
    return jnp.where((lane >= 16) & (lane < 24), tile[..., 128:], tile[..., :128])


def assemble(refs, lam_s, wide_s):
    lam_ref, winds_ref, from_cross, from_sibling = refs
    even = lax.rem(lax.axis_index("lon"), 2) == 0
    sub = iota((8, WIDE), 0)
    for row in range(-HALO, ROWS + HALO):
        at = ext_index(row)
        lam = lam_ref[at]
        sibling = from_sibling[at // 2].astype(F32)
        cross = from_cross[at // 2].astype(F32)
        east = jnp.where(even, sibling, cross)
        west = jnp.where(even, cross, sibling)
        odd = at % 2
        east_lam, west_lam = east[0:8], west[0:8]
        if not odd:
            east_lam, west_lam = pltpu.roll(east_lam, 4, 0), pltpu.roll(west_lam, 4, 0)
        lam_s[at, 0:8] = lam[0:8]
        lam_s[at, 8:16] = jnp.where(sub < 4, lam[8:16], east_lam)
        lam_s[at, 16:24] = west_lam
        east_wind, west_wind = (side[8:16, 128 * odd : 128 * odd + 128] for side in (east, west))
        east_wind, west_wind = (
            jnp.concatenate([main, pltpu.roll(side[0:8, 128:], 128 - SPARE[odd], 1)], axis=1)
            for main, side in ((east_wind, east), (west_wind, west))
        )
        for step in range(1, 5):
            reach = HALO - step
            if not -reach <= row < ROWS + reach:
                continue
            place = wind_index(step, row)
            wind = winds_ref[place].astype(F32)
            ew, ww = east_wind, west_wind
            if step == 2:
                ew, ww = pltpu.roll(ew, 4, 0), pltpu.roll(ww, 4, 0)
            if step == 3:
                ew, ww = pltpu.roll(ew, 2, 0), pltpu.roll(ww, 6, 0)
            wide_s[place, 0:16] = jnp.concatenate(
                [wind[0:8], jnp.where(sub < 4, wind[8:16], ew)], axis=0
            ).astype(BF16)
            wide_s[place, 16:24] = ww.astype(BF16)


def wind_spread(narrow):
    lanes = 128 if narrow else WIDE
    source = iota((lanes, 2 * lanes), 0)
    lane = iota((lanes, 2 * lanes), 1)
    second = lane >= lanes
    lane = jnp.where(second, lane - lanes, lane)
    if narrow:
        level = jnp.where(lane >= LEVELS, lane - LEVELS, jnp.where(lane >= 16, lane - 16, lane))
        used = level < 8
    else:
        level = lane - jnp.where(lane >= LEVELS, LEVELS, 0) - jnp.where(lane >= 2 * LEVELS, LEVELS, 0)
        used = lane < WIDTH
    match = (source == level + jnp.where(second, LEVELS, 0)) & used
    return jnp.where(match, 0.5, 0.0).astype(BF16)


def advance(lam_a, lam_b, wide_s, coef_s, narrow, emit):
    lat = lax.axis_index("lat")
    has_south = jnp.where(lat > 0, 1.0, 0.0).astype(F32)
    has_north = jnp.where(lat < lax.axis_size("lat") - 1, 1.0, 0.0).astype(F32)
    cols = SUB + 8
    lanes = 128 if narrow else WIDE
    spread = wind_spread(narrow)
    lane = iota((cols, lanes), 1)
    if narrow:
        top = None
        bottom = (lane == 0) | (lane == 16) | (lane == LEVELS)
    else:
        top = (lane == LEVELS - 1) | (lane == 2 * LEVELS - 1) | (lane == 3 * LEVELS - 1)
        bottom = (lane == 0) | (lane == LEVELS) | (lane == 2 * LEVELS)
    now, later = lam_a, lam_b
    for step in range(1, 5):
        reach = HALO - step
        count = ROWS + 2 * reach
        base = wind_index(step, 0)
        lhs = wide_s[base : base + count].reshape(count * cols, lanes)
        coef_s[:count] = jnp.dot(lhs, spread, preferred_element_type=F32).reshape(count, cols, 2 * lanes)
        for row in range(-reach, ROWS + reach):
            at = ext_index(row)
            mid = now[at]
            north = now[ext_index(row + 1)]
            south = now[ext_index(row - 1)]
            east = pltpu.roll(mid, cols - 1, 0)
            west = pltpu.roll(mid, 1, 0)
            upper = pltpu.roll(mid, lanes - 1, 1)
            if top is not None:
                upper = jnp.where(top, mid, upper)
            lower = jnp.where(bottom, mid, pltpu.roll(mid, 1, 1))
            place = wind_index(step, row) - base
            u = coef_s[place, :, :lanes]
            v = coef_s[place, :, lanes:]
            new = (
                CENTER * mid
                + u * (east - west)
                + v * (north - south)
                + HORIZ_MIX * ((east + west) + (north + south))
                + VERT_MIX * (upper + lower)
            )
            if row < 0:
                new = new * has_south
            if row >= ROWS:
                new = new * has_north
            if step < 4:
                later[at] = new
            if 0 <= row < ROWS:
                emit(step, row, new)
        now, later = later, now


def assemble_low(refs, lam_s, wide_s):
    lam_ref, from_south, from_north, winds_ref, from_cross, from_sibling = refs
    sub = iota((8, 128), 0)
    halos = []
    for strip in (from_south, from_north):
        halves = [strip[i].astype(F32) for i in range(STRIP)]
        halos.append((*unpack_strip(halves), halves[9][8:16], halves[10][8:16]))
    for row in range(-HALO, ROWS + HALO):
        own = 0 <= row < ROWS
        at = ext_index(row)
        if own:
            lam = pack_low(lam_ref[row])
            sides = edge_winds(from_cross, from_sibling, row)
        else:
            lam_rows, wind_rows, east, west = halos[0 if row < 0 else 1]
            lam = pack_low(lam_rows[row + HALO if row < 0 else row - ROWS])
        lam_s[at, 0:8] = lam[0:8]
        lam_s[at, 8:16] = jnp.where(sub < 4, lam[8:16], 0.0)
        lam_s[at, 16:24] = jnp.zeros((8, 128), F32)
        for step in range(1, 5):
            reach = HALO - step
            if not -reach <= row < ROWS + reach:
                continue
            if own:
                wind = winds_ref[4 - step, row, :, :128].astype(F32)
                east_wind, west_wind = sides[0][step], sides[1][step]
            else:
                index = WIND_FIRST[step] + (row + reach if row < 0 else row - ROWS)
                wind = wind_rows[index][:, :128]
                east_wind, west_wind = (pltpu.roll(side, 128 - 4 * index, 1) if index else side for side in (east, west))
            place = wind_index(step, row)
            wide_s[place, 0:16] = jnp.concatenate(
                [wind[0:8], jnp.where(sub < 4, wind[8:16], east_wind)], axis=0
            ).astype(BF16)
            wide_s[place, 16:24] = west_wind.astype(BF16)


LOW = WIDTH // 6


def surface_body(
    lam_ref, from_south, from_north, winds_ref, from_cross, from_sibling, out_ref, lam_a, lam_b, wide_s, coef_s, acc_s
):
    assemble_low((lam_ref, from_south, from_north, winds_ref, from_cross, from_sibling), lam_a, wide_s)

    def emit(step, row, value):
        acc_s[row] = value if step == 1 else acc_s[row] + value

    advance(lam_a, lam_b, wide_s, coef_s, True, emit)
    lane = iota((SUB + 8, 128), 1)
    surface = jnp.zeros((SUB + 8, 128), F32)
    for row in range(ROWS):
        held = acc_s[row]
        for species, source in enumerate((0, LEVELS, 16)):
            at = row * SPECIES + species
            surface = jnp.where(lane == at, pltpu.roll(held, (at - source) % 128, 1), surface)
    high = surface.astype(BF16).astype(F32)
    low = (surface - high).astype(BF16).astype(F32)
    lane = iota((8, 128), 1)
    parts = []
    for tile, last in ((0, high), (1, low)):
        cut = slice(8 * tile, 8 * tile + 8)
        second = pltpu.roll(low[cut], LOW, 1)
        third = pltpu.roll(last[16:24], 2 * LOW, 1)
        parts.append(jnp.where(lane < LOW, high[cut], jnp.where(lane < 2 * LOW, second, third)))
    block = jnp.concatenate(parts, axis=0).astype(BF16)
    for target in range(out_ref.shape[0] // SUB):
        out_ref[SUB * target : SUB * target + SUB] = block


def steps_body(lam_ref, winds_ref, from_cross, from_sibling, field_ref, lam_a, lam_b, wide_s, coef_s):
    refs = (lam_ref, winds_ref, from_cross, from_sibling)
    assemble(refs, lam_a, wide_s)

    def emit(step, row, value):
        if step == 4:
            field_ref[row] = value[:ROWS, :WIDTH]

    advance(lam_a, lam_b, wide_s, coef_s, False, emit)


def correlation_body(correlation_ref, out_ref):
    total = correlation_ref.shape[1]
    length = total // ROWS * 8
    source = iota((total, length), 0)
    block = iota((total, length), 1) >> 3
    place = iota((total, length), 1) & 7
    first = source == block * ROWS + place
    second = (source == block * ROWS + 8 + place) & (place < 4)
    for index, match in enumerate((first, second)):
        pick = jnp.where(match, 1.0, 0.0).astype(BF16)
        part = jnp.dot(correlation_ref[...], pick, preferred_element_type=F32)
        part = jnp.concatenate([part, jnp.zeros((SUB - ROWS, length), F32)], axis=0)
        out_ref[SUB * index : SUB * index + SUB] = part.astype(BF16)


def gradient_body(surface_ref, correlation_ref, out_ref, blocks_s):
    blocks = surface_ref.shape[0] // SUB
    lane = iota((8, 128), 1)
    sub = iota((8, 128), 0)
    mains, easts, wests = [], [], []
    for block in range(blocks):
        both = surface_ref[SUB * block : SUB * block + SUB].astype(F32)
        whole = both + pltpu.roll(both, 128 - LOW, 1)
        mains.append(whole)
        easts.append(pltpu.roll(whole[8:16], 4, 0))
        wests.append(pltpu.roll(pltpu.roll(both[0:8] + both[8:16], 128 - 2 * LOW, 1), 4, 0))
    for pair in range(blocks // 2):
        parts = []
        for block in (2 * pair, 2 * pair + 1):
            left = mains[block][0:8] + jnp.where(sub < 4, easts[block - 1], 0.0)
            right = jnp.where(sub < 4, mains[block][8:16] + wests[(block + 1) % blocks], 0.0)
            parts.append(jnp.where(lane < 64, left, pltpu.roll(right, 64, 1)))
        blocks_s[SUB * pair : SUB * pair + SUB] = jnp.concatenate(parts, axis=0).astype(BF16)
    both = jnp.dot(correlation_ref[...], blocks_s[...], preferred_element_type=F32)
    sums = both[:SUB] + pltpu.roll(both[SUB:], 64, 1)
    result = jnp.transpose(sums)
    for row in range(ROWS):
        out_ref[row] = result[SPECIES * row : SPECIES * row + SPECIES, :ROWS]


def per_device(
    adjoint_in, stored_winds, innovations, columns, kernel_ids, counts, offsets, kernel_table, correlation
):
    lon_count = lax.axis_size("lon")
    lat_count = lax.axis_size("lat")
    shape = jax.ShapeDtypeStruct
    held = innovations.shape[2]
    sent = vmem_call(
        route_body,
        shape((lon_count * CAP, WIDE), BF16),
        [
            pltpu.VMEM((1, lon_count), jnp.int32),
            pltpu.VMEM((1, lon_count), jnp.int32),
            pltpu.VMEM((1, held), jnp.int32),
            pltpu.VMEM((1, held), jnp.int32),
            pltpu.VMEM((WIDTH, held), BF16),
            pltpu.SemaphoreType.DMA((5,)),
        ],
        name="route",
        limit=63 * 1000 * 1000,
        in_specs=[pl.BlockSpec(memory_space=pltpu.HBM)] * 5,
    )(counts, offsets, columns, kernel_ids, jnp.swapaxes(innovations, 2, 3))
    recv = lax.all_to_all(sent, "lon", split_axis=0, concat_axis=0, tiled=True)
    rim = shape((SUB, 128), BF16)
    winds, rim_sibling, rim_cross = vmem_call(
        winds_body, (shape((4, ROWS, SUB, WIDE), BF16), rim, rim), name="winds"
    )(stored_winds)
    across = [(i, (i + (1 if i % 2 else -1)) % lon_count) for i in range(lon_count)]
    within = [(i, i ^ 1) for i in range(lon_count)]
    winds_cross = lax.ppermute(rim_cross, "lon", across)
    winds_sibling = lax.ppermute(rim_sibling, "lon", within)
    turned = vmem_call(correlation_body, shape((2 * SUB, lon_count * 8), BF16), name="correlation")(correlation.T)
    strip = shape((STRIP, SUB, 128), BF16)
    lam, north, south = vmem_call(
        force_body,
        (shape((ROWS, SUB, WIDE), F32), strip, strip),
        [pltpu.VMEM((3 * kernel_table.shape[0], WIDE), BF16)],
        name="force",
    )(recv, kernel_table, adjoint_in, winds, winds_cross, winds_sibling)
    up = [(i, i + 1) for i in range(lat_count - 1)]
    down = [(i + 1, i) for i in range(lat_count - 1)]
    from_south = lax.ppermute(north, "lat", up)
    from_north = lax.ppermute(south, "lat", down)
    cols = SUB + 8

    def scratch(lanes):
        return [
            pltpu.VMEM((EXT, cols, lanes), F32),
            pltpu.VMEM((EXT, cols, lanes), F32),
            pltpu.VMEM((60, cols, lanes), BF16),
            pltpu.VMEM((EXT, cols, 2 * lanes), F32),
        ]

    surface = vmem_call(
        surface_body,
        shape((lon_count * SUB, 128), BF16),
        scratch(128) + [pltpu.VMEM((ROWS, cols, 128), F32)],
        name="surface",
    )(lam, from_south, from_north, winds, winds_cross, winds_sibling)
    gathered = lax.all_to_all(surface, "lon", split_axis=0, concat_axis=0, tiled=True)
    edge = shape((EXT // 2, SUB, WIDE), BF16)
    to_sibling, to_cross, lam_ext, winds_ext = vmem_call(
        edge_body,
        (edge, edge, shape((EXT, SUB, WIDE), F32), shape((60, SUB, WIDE), BF16)),
        name="edge",
        in_specs=[pl.BlockSpec(memory_space=pltpu.VMEM)] * 4 + [pl.BlockSpec(memory_space=pl.ANY)],
    )(lam, from_south, from_north, winds, surface)
    from_cross = lax.ppermute(to_cross, "lon", across)
    from_sibling = lax.ppermute(to_sibling, "lon", within)
    state = (lam_ext, winds_ext, from_cross, from_sibling)
    gradient = vmem_call(
        gradient_body,
        shape((ROWS, SPECIES, ROWS), F32),
        [pltpu.VMEM((lon_count * 8, 128), BF16)],
        name="gradient",
    )(gathered, turned)
    field = vmem_call(
        steps_body,
        shape((ROWS, ROWS, WIDTH), F32),
        scratch(WIDE),
        name="steps",
    )(*state)
    return field, gradient


def solution(mesh):
    return jax.shard_map(
        per_device,
        mesh=mesh,
        in_specs=(
            P("lat", "lon", None),
            P(None, "lat", "lon", None),
            P("lat", "lon", None, None),
            P("lat", "lon", None),
            P("lat", "lon", None),
            P("lat", "lon", None),
            P("lat", "lon", None),
            P(),
            P(None, "lon"),
        ),
        out_specs=(P("lat", "lon", None), P("lat", None, "lon")),
        check_vma=False,
    )
```

```python
import functools

import jax
import jax.numpy as jnp
from jax import lax
from jax.experimental import pallas as pl
from jax.experimental.pallas import tpu as pltpu
from jax.sharding import PartitionSpec as P

CAP = 8
HORIZ_MIX = 0.18
VERT_MIX = 0.1
CENTER = 1.0 - 4.0 * HORIZ_MIX - 2.0 * VERT_MIX

ROWS = 12
HALO = 4
SUB = 16
WIDE = 256
LEVELS = 72
SPECIES = 3
WIDTH = SPECIES * LEVELS
CODE_LANE = 216
KERNEL_LANE = 217
F32 = jnp.float32
BF16 = jnp.bfloat16


def iota(shape, dim):
    return lax.broadcasted_iota(jnp.int32, shape, dim)


def vmem_call(body, outs, scratch=(), name=None, limit=48 * 1024 * 1024, **specs):
    return pl.pallas_call(
        body,
        out_shape=outs,
        scratch_shapes=list(scratch),
        name=name,
        compiler_params=pltpu.CompilerParams(vmem_limit_bytes=limit),
        **specs,
    )


def route_body(
    counts_hbm, offsets_hbm, columns_hbm, kernels_hbm, innov_hbm, out_ref,
    counts_s, offsets_s, columns_s, kernels_s, innov_s, sems,
):
    moves = (
        (counts_hbm.at[0], counts_s),
        (offsets_hbm.at[0], offsets_s),
        (columns_hbm.at[0], columns_s),
        (kernels_hbm.at[0], kernels_s),
        (innov_hbm.at[0, 0], innov_s),
    )
    copies = [pltpu.make_async_copy(source, target, sems.at[i]) for i, (source, target) in enumerate(moves)]
    for copy in copies:
        copy.start()
    for copy in copies[:4]:
        copy.wait()
    held = innov_s.shape[1]
    owners = counts_s.shape[1]
    eye = iota((owners, owners), 0) == iota((owners, owners), 1)
    offset_col = jnp.sum(jnp.where(eye, offsets_s[...].astype(F32), 0.0), axis=1, keepdims=True)
    count_col = jnp.sum(jnp.where(eye, counts_s[...].astype(F32), 0.0), axis=1, keepdims=True)
    place = iota((owners, held), 1).astype(F32) - offset_col
    place = jnp.where(place < count_col, place, -1.0)
    slot = iota((owners, CAP, held), 1).astype(F32)
    pick = jnp.where(place[:, None, :] == slot, 1.0, 0.0).reshape(owners * CAP, held).astype(BF16)
    cell = columns_s[...]
    code = (cell + 4 * ((cell * 171) >> 11) + 1).astype(F32)
    half = WIDE // 2
    line = iota((half, held), 0)
    codes = jnp.where(
        line == CODE_LANE - half,
        code,
        jnp.where(line == KERNEL_LANE - half, kernels_s[...].astype(F32), 0.0),
    ).astype(BF16)
    tail = lax.dot_general(pick, codes, (((1,), (1,)), ((), ())), preferred_element_type=F32)
    out_ref[:, half:] = tail.astype(BF16)
    copies[4].wait()
    sent = lax.dot_general(
        pick, innov_s[...], (((1,), (1,)), ((), ())), preferred_element_type=F32
    ).astype(BF16)
    out_ref[:, :half] = sent[:, :half]
    out_ref[:, half:WIDTH] = sent[:, half:]


def pack_levels(tiles):
    lane = iota(tiles[0].shape, 1)
    lane = jnp.where(lane >= LEVELS, lane - LEVELS, lane)
    packed = tiles[0]
    for index in range(1, len(tiles)):
        packed = jnp.where(lane >= 4 * index, pltpu.roll(tiles[index], 4 * index, 1), packed)
    return packed


def winds_body(winds_ref, out_ref, sibling_ref, cross_ref):
    out_ref[...] = jnp.zeros_like(out_ref)
    out_ref[:, :, :ROWS, : 2 * LEVELS] = winds_ref[...]
    even = lax.rem(lax.axis_index("lon"), 2) == 0
    sub = iota((8, 128), 0)
    made = []
    for tile in (1, 0):
        rows = []
        for row in range(ROWS):
            cuts = [out_ref[4 - step, row, :, :128].astype(F32)[8 * tile : 8 * tile + 8] for step in (1, 2, 3, 4)]
            parts = [jnp.where(sub < 4, cuts[i], pltpu.roll(cuts[i + 1], 4, 0)) for i in (0, 2)]
            rows.append(jnp.concatenate(parts, axis=0))
        made.append(pack_levels(rows))
    to_east, to_west = made
    sibling_ref[...] = jnp.where(even, to_east, to_west).astype(BF16)
    cross_ref[...] = jnp.where(even, to_west, to_east).astype(BF16)


def edge_winds(from_cross, from_sibling, row):
    even = lax.rem(lax.axis_index("lon"), 2) == 0
    sibling = from_sibling[...].astype(F32)
    cross = from_cross[...].astype(F32)
    sides = []
    for side in (jnp.where(even, sibling, cross), jnp.where(even, cross, sibling)):
        if row:
            side = pltpu.roll(side, 128 - 4 * row, 1)
        first, second = side[0:8], side[8:16]
        sides.append({1: pltpu.roll(first, 4, 0), 2: first, 3: pltpu.roll(second, 4, 0), 4: second})
    return sides


STRIP = 11
SPARE = (WIDTH - 128, WIDTH - 112)


def pieces(row):
    return pltpu.roll(row[0:8], 4, 0), row[0:8], pltpu.roll(row[8:16], 4, 0)


def with_piece(row, piece):
    sub = iota((8, row.shape[1]), 0)
    return jnp.concatenate([row[0:8], jnp.where(sub < 4, row[8:16], piece)], axis=0)


def pack_strip(lam_rows, wind_rows, east, west):
    extra = pieces(lam_rows[3])
    lane = iota((SUB, 128), 1)
    halves = []
    for index in range(3):
        packed = with_piece(lam_rows[index], extra[index])
        one, two = (pltpu.roll(wind_rows[index + 3 * i][:, 128:], SPARE[i], 1) for i in range(2))
        halves += [
            packed[:, :128],
            jnp.where(lane < SPARE[0], packed[:, 128:], jnp.where(lane < SPARE[1], one, two)),
        ]
    main = [row[:, :128] for row in wind_rows]
    extra = pieces(main[4])
    halves += [with_piece(main[index], extra[index]) for index in range(3)]
    halves += [with_piece(main[3], pack_levels(east)), with_piece(main[5], pack_levels(west))]
    return halves


def rejoin(tiles):
    first, second, third = (tile[8:16] for tile in tiles)
    sub = iota(first.shape, 0)
    return jnp.concatenate([jnp.where(sub < 4, pltpu.roll(first, 4, 0), second), pltpu.roll(third, 4, 0)], axis=0)


def unpack_strip(halves):
    tiles = [jnp.concatenate(halves[2 * i : 2 * i + 2], axis=1) for i in range(3)]
    lam_rows = tiles + [rejoin(tiles)]
    main = halves[6:10] + [rejoin(halves[6:9]), halves[10]]
    wind_rows = []
    for index in range(6):
        last = pltpu.roll(halves[2 * (index % 3) + 1], 128 - SPARE[index // 3], 1)
        wind_rows.append(jnp.concatenate([main[index], last], axis=1))
    return lam_rows, wind_rows


def force_body(
    recv_ref, table_ref, adjoint_ref, winds_ref, from_cross, from_sibling, lam_ref, north_ref, south_ref, table_s
):
    total = recv_ref.shape[0]
    nkernel = table_ref.shape[0]
    recv = recv_ref[...]
    wide = recv.astype(F32)
    pick = jnp.where((iota((8, WIDE), 1) == CODE_LANE), 1.0, 0.0).astype(BF16)
    code_line = lax.dot_general(pick, recv, (((1,), (1,)), ((), ())), preferred_element_type=F32)
    kernel_col = wide[:, KERNEL_LANE : KERNEL_LANE + 1]
    lane = iota((total, 3 * nkernel), 1)
    lane = (lane - jnp.where(lane >= nkernel, nkernel, 0) - jnp.where(lane >= 2 * nkernel, nkernel, 0)).astype(F32)
    onehot = jnp.where(kernel_col == lane, 1.0, 0.0).astype(BF16)
    table = table_ref[...]
    table_s[...] = jnp.zeros_like(table_s)
    high = table.astype(BF16)
    rest = table - high.astype(F32)
    middle = rest.astype(BF16)
    table_s[0:nkernel, :WIDTH] = high
    table_s[nkernel : 2 * nkernel, :WIDTH] = middle
    table_s[2 * nkernel :, :WIDTH] = (rest - middle.astype(F32)).astype(BF16)
    weights = jnp.dot(onehot, table_s[...], preferred_element_type=F32)
    weighted = wide * weights
    whigh = weighted.astype(BF16)
    wlow = (weighted - whigh.astype(F32)).astype(BF16)
    cell = (iota((ROWS * SUB, total), 0) + 1).astype(F32)
    scatter = jnp.where(cell == code_line[0:1, :], 1.0, 0.0).astype(BF16)
    force = jnp.dot(scatter, whigh, preferred_element_type=F32) + jnp.dot(
        scatter, wlow, preferred_element_type=F32
    )
    lam_ref[...] = force.reshape(ROWS, SUB, WIDE)
    lam_ref[:, :ROWS, :WIDTH] = lam_ref[:, :ROWS, :WIDTH] + adjoint_ref[...]
    for lower, strip in ((False, north_ref), (True, south_ref)):
        start = 0 if lower else ROWS - HALO
        wind_rows, east, west = [], [], []
        for step in (1, 2, 3):
            depth = HALO - step
            begin = 0 if lower else ROWS - depth
            for row in range(begin, begin + depth):
                wind_rows.append(winds_ref[4 - step, row].astype(F32))
                sides = edge_winds(from_cross, from_sibling, row)
                east.append(sides[0][step])
                west.append(sides[1][step])
        for index, half in enumerate(pack_strip([lam_ref[start + i] for i in range(HALO)], wind_rows, east, west)):
            strip[index] = half.astype(BF16)


WIND_FIRST = {1: 0, 2: 3, 3: 5}
EXT = ROWS + 2 * HALO


def ext_index(row):
    return row if row >= 0 else row + EXT


def wind_index(step, row):
    base = (0, 18, 34, 48)[step - 1]
    reach = HALO - step
    return base + (row if row >= 0 else row + ROWS + 2 * reach)


def edge_body(lam_ref, from_south, from_north, winds_ref, _, sibling_ref, cross_ref, lam_out, winds_out):
    south_lam, south_winds = unpack_strip([from_south[i].astype(F32) for i in range(STRIP)])
    north_lam, north_winds = unpack_strip([from_north[i].astype(F32) for i in range(STRIP)])
    even = lax.rem(lax.axis_index("lon"), 2) == 0
    sub = iota((8, WIDE), 0)
    lane = iota((8, 128), 1)
    none = jnp.zeros((SUB, WIDE), F32)
    held = {}
    for row in sorted(range(-HALO, ROWS + HALO), key=ext_index):
        own = 0 <= row < ROWS
        lam = lam_ref[row] if own else (south_lam[row + HALO] if row < 0 else north_lam[row - ROWS])
        lam_out[ext_index(row)] = lam
        wind = {}
        for step in (1, 2, 3, 4):
            reach = HALO - step
            if own:
                raw = winds_ref[4 - step, row]
                winds_out[wind_index(step, row)] = raw
                wind[step] = raw.astype(F32)
            elif -reach <= row < ROWS + reach:
                rows, at = (south_winds, row + reach) if row < 0 else (north_winds, row - ROWS)
                wind[step] = rows[WIND_FIRST[step] + at]
                winds_out[wind_index(step, row)] = wind[step].astype(BF16)
            else:
                wind[step] = none
        made = []
        for tile in (1, 0):
            cut = slice(8 * tile, 8 * tile + 8)
            upper = pltpu.roll(wind[1][cut], 4, 0)
            if tile == 1:
                rest = jnp.where(sub >= 2, wind[2][cut], pltpu.roll(wind[3][cut], 6, 0))
            else:
                rest = jnp.where(sub < 2, wind[2][cut], pltpu.roll(wind[3][cut], 2, 0))
            made.append((lam[cut], jnp.where(sub >= 4, upper, rest)))
        if ext_index(row) % 2 == 0:
            held = made
            continue
        strips = []
        for (lam_a, wind_a), (lam_b, wind_b) in zip(held, made, strict=True):
            both = jnp.where(sub < 4, lam_a, pltpu.roll(lam_b, 4, 0))
            one = pltpu.roll(wind_a[:, 128:], SPARE[0], 1)
            two = pltpu.roll(wind_b[:, 128:], SPARE[1], 1)
            last = jnp.where(lane < SPARE[0], both[:, 128:], jnp.where(lane < SPARE[1], one, two))
            upper = jnp.concatenate([both[:, :128], last], axis=1)
            lower = jnp.concatenate([wind_a[:, :128], wind_b[:, :128]], axis=1)
            strips.append(jnp.concatenate([upper, lower], axis=0))
        to_east, to_west = strips
        sibling_ref[ext_index(row) // 2] = jnp.where(even, to_east, to_west).astype(BF16)
        cross_ref[ext_index(row) // 2] = jnp.where(even, to_west, to_east).astype(BF16)


def assemble(refs, lam_s, wide_s):
    lam_ref, winds_ref, from_cross, from_sibling = refs
    even = lax.rem(lax.axis_index("lon"), 2) == 0
    sub = iota((8, WIDE), 0)
    for row in range(-HALO, ROWS + HALO):
        at = ext_index(row)
        lam = lam_ref[at]
        sibling = from_sibling[at // 2].astype(F32)
        cross = from_cross[at // 2].astype(F32)
        east = jnp.where(even, sibling, cross)
        west = jnp.where(even, cross, sibling)
        odd = at % 2
        east_lam, west_lam = east[0:8], west[0:8]
        if not odd:
            east_lam, west_lam = pltpu.roll(east_lam, 4, 0), pltpu.roll(west_lam, 4, 0)
        lam_s[at, 0:8] = lam[0:8]
        lam_s[at, 8:16] = jnp.where(sub < 4, lam[8:16], east_lam)
        lam_s[at, 16:24] = west_lam
        east_wind, west_wind = (side[8:16, 128 * odd : 128 * odd + 128] for side in (east, west))
        east_wind, west_wind = (
            jnp.concatenate([main, pltpu.roll(side[0:8, 128:], 128 - SPARE[odd], 1)], axis=1)
            for main, side in ((east_wind, east), (west_wind, west))
        )
        for step in range(1, 5):
            reach = HALO - step
            if not -reach <= row < ROWS + reach:
                continue
            place = wind_index(step, row)
            wind = winds_ref[place].astype(F32)
            ew, ww = east_wind, west_wind
            if step == 2:
                ew, ww = pltpu.roll(ew, 4, 0), pltpu.roll(ww, 4, 0)
            if step == 3:
                ew, ww = pltpu.roll(ew, 2, 0), pltpu.roll(ww, 6, 0)
            wide_s[place, 0:16] = jnp.concatenate(
                [wind[0:8], jnp.where(sub < 4, wind[8:16], ew)], axis=0
            ).astype(BF16)
            wide_s[place, 16:24] = ww.astype(BF16)


def wind_spread():
    source = iota((WIDE, 2 * WIDE), 0)
    lane = iota((WIDE, 2 * WIDE), 1)
    second = lane >= WIDE
    lane = jnp.where(second, lane - WIDE, lane)
    level = lane - jnp.where(lane >= LEVELS, LEVELS, 0) - jnp.where(lane >= 2 * LEVELS, LEVELS, 0)
    match = (source == level + jnp.where(second, LEVELS, 0)) & (lane < WIDTH)
    return jnp.where(match, 0.5, 0.0).astype(BF16)


def poles():
    lat = lax.axis_index("lat")
    has_south = jnp.where(lat > 0, 1.0, 0.0).astype(F32)
    return has_south, jnp.where(lat < lax.axis_size("lat") - 1, 1.0, 0.0).astype(F32)


def updated(mid, north, south, u, v, top, bottom):
    cols, lanes = mid.shape
    east = pltpu.roll(mid, cols - 1, 0)
    west = pltpu.roll(mid, 1, 0)
    upper = pltpu.roll(mid, lanes - 1, 1)
    if top is not None:
        upper = jnp.where(top, mid, upper)
    lower = jnp.where(bottom, mid, pltpu.roll(mid, 1, 1))
    return (
        CENTER * mid
        + u * (east - west)
        + v * (north - south)
        + HORIZ_MIX * ((east + west) + (north + south))
        + VERT_MIX * (upper + lower)
    )


def advance(lam_a, lam_b, wide_s, coef_s, field_ref):
    has_south, has_north = poles()
    cols = SUB + 8
    spread = wind_spread()
    lane = iota((cols, WIDE), 1)
    top = (lane == LEVELS - 1) | (lane == 2 * LEVELS - 1) | (lane == 3 * LEVELS - 1)
    bottom = (lane == 0) | (lane == LEVELS) | (lane == 2 * LEVELS)
    now, later = lam_a, lam_b
    for step in range(1, 5):
        reach = HALO - step
        count = ROWS + 2 * reach
        base = wind_index(step, 0)
        lhs = wide_s[base : base + count].reshape(count * cols, WIDE)
        coef_s[base : base + count] = jnp.dot(lhs, spread, preferred_element_type=F32).reshape(count, cols, 2 * WIDE)
        for row in range(-reach, ROWS + reach):
            place = wind_index(step, row)
            new = updated(
                now[ext_index(row)], now[ext_index(row + 1)], now[ext_index(row - 1)],
                coef_s[place, :, :WIDE], coef_s[place, :, WIDE:], top, bottom,
            )
            if row < 0:
                new = new * has_south
            if row >= ROWS:
                new = new * has_north
            if step < 4:
                later[ext_index(row)] = new
            else:
                field_ref[row] = new[:ROWS, :WIDTH]
        now, later = later, now


GROUP = EXT // 4
SPECIES_LANES = 8


def low_levels(tile):
    lane = iota((8, 128), 1)
    first = tile[:, :128]
    low = jnp.where(
        lane < SPECIES_LANES,
        first,
        jnp.where(lane < 2 * SPECIES_LANES, pltpu.roll(first, 128 - LEVELS + SPECIES_LANES, 1), tile[:, 128:]),
    )
    return jnp.where(lane < SPECIES * SPECIES_LANES, low, 0.0)


def assemble_low(refs, lam_s, wide_s):
    lam_ref, from_south, from_north, winds_ref, from_cross, from_sibling = refs
    sub = iota((8, 128), 0)
    halos = []
    for strip in (from_south, from_north):
        halves = [strip[i].astype(F32) for i in range(STRIP)]
        halos.append((*unpack_strip(halves), halves[9][8:16], halves[10][8:16]))
    held = [[jnp.zeros((8, 128), F32)] * 2 for _ in range(GROUP)]
    for row in range(-HALO, ROWS + HALO):
        own = 0 <= row < ROWS
        group, at = divmod(row + HALO, GROUP)
        if own:
            lam = lam_ref[row]
            sides = edge_winds(from_cross, from_sibling, row)
        else:
            lam_rows, wind_rows, east, west = halos[0 if row < 0 else 1]
            lam = lam_rows[row + HALO if row < 0 else row - ROWS]
        for tile in range(2):
            low = low_levels(lam[8 * tile : 8 * tile + 8])
            held[at][tile] = held[at][tile] + (pltpu.roll(low, 32 * group, 1) if group else low)
        lanes = slice(128 * group, 128 * group + 128)
        for step in range(1, 5):
            reach = HALO - step
            place = (step - 1) * GROUP + at
            if not -reach <= row < ROWS + reach:
                wide_s[place, :, lanes] = jnp.zeros((SUB + 8, 128), BF16)
                continue
            if own:
                wind = winds_ref[4 - step, row, :, :128].astype(F32)
                east_wind, west_wind = sides[0][step], sides[1][step]
            else:
                index = WIND_FIRST[step] + (row + reach if row < 0 else row - ROWS)
                wind = wind_rows[index][:, :128]
                east_wind, west_wind = (pltpu.roll(side, 128 - 4 * index, 1) if index else side for side in (east, west))
            wide_s[place, 0:16, lanes] = jnp.concatenate(
                [wind[0:8], jnp.where(sub < 4, wind[8:16], east_wind)], axis=0
            ).astype(BF16)
            wide_s[place, 16:24, lanes] = west_wind.astype(BF16)
    for at in range(GROUP):
        lam_s[at, 0:8] = held[at][0]
        lam_s[at, 8:16] = jnp.where(sub < 4, held[at][1], 0.0)
        lam_s[at, 16:24] = jnp.zeros((8, 128), F32)


def low_spread():
    source = iota((4 * 128, 2 * 128), 0)
    lane = iota((4 * 128, 2 * 128), 1)
    level = lane & (SPECIES_LANES - 1)
    wanted = ((lane & 127) >> 5) * 128 + level + jnp.where(lane >= 128, LEVELS, 0)
    match = (source == wanted) & (level < 4) & ((lane & 31) < SPECIES * SPECIES_LANES)
    return jnp.where(match, 0.5, 0.0).astype(BF16)


def advance_low(lam_a, lam_b, wide_s, coef_s, acc_s):
    has_south, has_north = poles()
    cols = SUB + 8
    spread = low_spread()
    lane = iota((cols, 128), 1)
    bottom = (lane & (SPECIES_LANES - 1)) == 0
    lhs = wide_s[...].reshape(4 * GROUP * cols, 4 * 128)
    coef_s[...] = jnp.dot(lhs, spread, preferred_element_type=F32).reshape(4 * GROUP, cols, 2 * 128)
    now, later = lam_a, lam_b
    for step in range(1, 5):
        for at in range(GROUP):
            place = (step - 1) * GROUP + at
            north = now[at + 1] if at < GROUP - 1 else pltpu.roll(now[0], 96, 1)
            south = now[at - 1] if at else pltpu.roll(now[GROUP - 1], 32, 1)
            new = updated(now[at], north, south, coef_s[place, :, :128], coef_s[place, :, 128:], None, bottom)
            if at < HALO:
                new = jnp.where(lane < 32, new * has_south, new)
            if at > 0:
                new = jnp.where(lane >= 96, new * has_north, new)
            later[at] = new
            acc_s[at] = new if step == 1 else acc_s[at] + new
        now, later = later, now


LOW = WIDTH // 6


def surface_body(
    lam_ref, from_south, from_north, winds_ref, from_cross, from_sibling, _, out_ref, lam_a, lam_b, wide_s, coef_s, acc_s
):
    assemble_low((lam_ref, from_south, from_north, winds_ref, from_cross, from_sibling), lam_a, wide_s)
    advance_low(lam_a, lam_b, wide_s, coef_s, acc_s)
    lane = iota((SUB + 8, 128), 1)
    surface = jnp.zeros((SUB + 8, 128), F32)
    for row in range(ROWS):
        group, place = divmod(row + HALO, GROUP)
        held = acc_s[place]
        for species in range(SPECIES):
            at = row * SPECIES + species
            source = 32 * group + SPECIES_LANES * species
            surface = jnp.where(lane == at, pltpu.roll(held, (at - source) % 128, 1), surface)
    high = surface.astype(BF16).astype(F32)
    low = (surface - high).astype(BF16).astype(F32)
    lane = iota((8, 128), 1)
    parts = []
    for tile, last in ((0, high), (1, low)):
        cut = slice(8 * tile, 8 * tile + 8)
        second = pltpu.roll(low[cut], LOW, 1)
        third = pltpu.roll(last[16:24], 2 * LOW, 1)
        parts.append(jnp.where(lane < LOW, high[cut], jnp.where(lane < 2 * LOW, second, third)))
    block = jnp.concatenate(parts, axis=0).astype(BF16)
    for target in range(out_ref.shape[0] // SUB):
        out_ref[SUB * target : SUB * target + SUB] = block


def steps_body(lam_ref, winds_ref, from_cross, from_sibling, field_ref, lam_a, lam_b, wide_s, coef_s):
    refs = (lam_ref, winds_ref, from_cross, from_sibling)
    assemble(refs, lam_a, wide_s)
    advance(lam_a, lam_b, wide_s, coef_s, field_ref)


def correlation_body(correlation_ref, out_ref):
    total = correlation_ref.shape[1]
    length = total // ROWS * 8
    source = iota((total, length), 0)
    block = iota((total, length), 1) >> 3
    place = iota((total, length), 1) & 7
    first = source == block * ROWS + place
    second = (source == block * ROWS + 8 + place) & (place < 4)
    for index, match in enumerate((first, second)):
        pick = jnp.where(match, 1.0, 0.0).astype(BF16)
        part = jnp.dot(correlation_ref[...], pick, preferred_element_type=F32)
        part = jnp.concatenate([part, jnp.zeros((SUB - ROWS, length), F32)], axis=0)
        out_ref[SUB * index : SUB * index + SUB] = part.astype(BF16)


def gradient_body(surface_ref, correlation_ref, out_ref, blocks_s):
    blocks = surface_ref.shape[0] // SUB
    lane = iota((8, 128), 1)
    sub = iota((8, 128), 0)
    mains, easts, wests = [], [], []
    for block in range(blocks):
        both = surface_ref[SUB * block : SUB * block + SUB].astype(F32)
        whole = both + pltpu.roll(both, 128 - LOW, 1)
        mains.append(whole)
        easts.append(pltpu.roll(whole[8:16], 4, 0))
        wests.append(pltpu.roll(pltpu.roll(both[0:8] + both[8:16], 128 - 2 * LOW, 1), 4, 0))
    for pair in range(blocks // 2):
        parts = []
        for block in (2 * pair, 2 * pair + 1):
            left = mains[block][0:8] + jnp.where(sub < 4, easts[block - 1], 0.0)
            right = jnp.where(sub < 4, mains[block][8:16] + wests[(block + 1) % blocks], 0.0)
            parts.append(jnp.where(lane < 64, left, pltpu.roll(right, 64, 1)))
        blocks_s[SUB * pair : SUB * pair + SUB] = jnp.concatenate(parts, axis=0).astype(BF16)
    both = jnp.dot(correlation_ref[...], blocks_s[...], preferred_element_type=F32)
    sums = both[:SUB] + pltpu.roll(both[SUB:], 64, 1)
    result = jnp.transpose(sums)
    for row in range(ROWS):
        out_ref[row] = result[SPECIES * row : SPECIES * row + SPECIES, :ROWS]


def per_device(
    adjoint_in, stored_winds, innovations, columns, kernel_ids, counts, offsets, kernel_table, correlation
):
    lon_count = lax.axis_size("lon")
    lat_count = lax.axis_size("lat")
    shape = jax.ShapeDtypeStruct
    held = innovations.shape[2]
    sent = vmem_call(
        route_body,
        shape((lon_count * CAP, WIDE), BF16),
        [
            pltpu.VMEM((1, lon_count), jnp.int32),
            pltpu.VMEM((1, lon_count), jnp.int32),
            pltpu.VMEM((1, held), jnp.int32),
            pltpu.VMEM((1, held), jnp.int32),
            pltpu.VMEM((WIDTH, held), BF16),
            pltpu.SemaphoreType.DMA((5,)),
        ],
        name="route",
        limit=63 * 1000 * 1000,
        in_specs=[pl.BlockSpec(memory_space=pltpu.HBM)] * 5,
    )(counts, offsets, columns, kernel_ids, jnp.swapaxes(innovations, 2, 3))
    recv = lax.all_to_all(sent, "lon", split_axis=0, concat_axis=0, tiled=True)
    rim = shape((SUB, 128), BF16)
    winds, rim_sibling, rim_cross = vmem_call(
        winds_body, (shape((4, ROWS, SUB, WIDE), BF16), rim, rim), name="winds"
    )(stored_winds)
    across = [(i, (i + (1 if i % 2 else -1)) % lon_count) for i in range(lon_count)]
    within = [(i, i ^ 1) for i in range(lon_count)]
    winds_cross = lax.ppermute(rim_cross, "lon", across)
    winds_sibling = lax.ppermute(rim_sibling, "lon", within)
    turned = vmem_call(correlation_body, shape((2 * SUB, lon_count * 8), BF16), name="correlation")(correlation.T)
    strip = shape((STRIP, SUB, 128), BF16)
    lam, north, south = vmem_call(
        force_body,
        (shape((ROWS, SUB, WIDE), F32), strip, strip),
        [pltpu.VMEM((3 * kernel_table.shape[0], WIDE), BF16)],
        name="force",
    )(recv, kernel_table, adjoint_in, winds, winds_cross, winds_sibling)
    up = [(i, i + 1) for i in range(lat_count - 1)]
    down = [(i + 1, i) for i in range(lat_count - 1)]
    from_south = lax.ppermute(north, "lat", up)
    from_north = lax.ppermute(south, "lat", down)
    cols = SUB + 8
    vmem = pl.BlockSpec(memory_space=pltpu.VMEM)
    surface = vmem_call(
        surface_body,
        shape((lon_count * SUB, 128), BF16),
        [
            pltpu.VMEM((GROUP, cols, 128), F32),
            pltpu.VMEM((GROUP, cols, 128), F32),
            pltpu.VMEM((4 * GROUP, cols, 4 * 128), BF16),
            pltpu.VMEM((4 * GROUP, cols, 2 * 128), F32),
            pltpu.VMEM((GROUP, cols, 128), F32),
        ],
        name="surface",
        in_specs=[vmem] * 6 + [pl.BlockSpec(memory_space=pl.ANY)],
    )(lam, from_south, from_north, winds, winds_cross, winds_sibling, turned)
    gathered = lax.all_to_all(surface, "lon", split_axis=0, concat_axis=0, tiled=True)
    edge = shape((EXT // 2, SUB, WIDE), BF16)
    to_sibling, to_cross, lam_ext, winds_ext = vmem_call(
        edge_body,
        (edge, edge, shape((EXT, SUB, WIDE), F32), shape((60, SUB, WIDE), BF16)),
        name="edge",
        in_specs=[vmem] * 4 + [pl.BlockSpec(memory_space=pl.ANY)],
    )(lam, from_south, from_north, winds, surface)
    from_cross = lax.ppermute(to_cross, "lon", across)
    from_sibling = lax.ppermute(to_sibling, "lon", within)
    state = (lam_ext, winds_ext, from_cross, from_sibling)
    gradient = vmem_call(
        gradient_body,
        shape((ROWS, SPECIES, ROWS), F32),
        [pltpu.VMEM((lon_count * 8, 128), BF16)],
        name="gradient",
    )(gathered, turned)
    field = vmem_call(
        steps_body,
        shape((ROWS, ROWS, WIDTH), F32),
        [
            pltpu.VMEM((EXT, cols, WIDE), F32),
            pltpu.VMEM((EXT, cols, WIDE), F32),
            pltpu.VMEM((60, cols, WIDE), BF16),
            pltpu.VMEM((60, cols, 2 * WIDE), F32),
        ],
        name="steps",
    )(*state)
    return field, gradient


def solution(mesh):
    return jax.shard_map(
        per_device,
        mesh=mesh,
        in_specs=(
            P("lat", "lon", None),
            P(None, "lat", "lon", None),
            P("lat", "lon", None, None),
            P("lat", "lon", None),
            P("lat", "lon", None),
            P("lat", "lon", None),
            P("lat", "lon", None),
            P(),
            P(None, "lon"),
        ),
        out_specs=(P("lat", "lon", None), P("lat", None, "lon")),
        check_vma=False,
    )
```

```python
import functools

import jax
import jax.numpy as jnp
from jax import lax
from jax.experimental import pallas as pl
from jax.experimental.pallas import tpu as pltpu
from jax.sharding import PartitionSpec as P

CAP = 8
HORIZ_MIX = 0.18
VERT_MIX = 0.1
CENTER = 1.0 - 4.0 * HORIZ_MIX - 2.0 * VERT_MIX

ROWS = 12
HALO = 4
SUB = 16
WIDE = 256
LEVELS = 72
SPECIES = 3
WIDTH = SPECIES * LEVELS
CODE_LANE = 216
KERNEL_LANE = 217
F32 = jnp.float32
BF16 = jnp.bfloat16


def iota(shape, dim):
    return lax.broadcasted_iota(jnp.int32, shape, dim)


def vmem_call(body, outs, scratch=(), name=None, limit=48 * 1024 * 1024, **specs):
    return pl.pallas_call(
        body,
        out_shape=outs,
        scratch_shapes=list(scratch),
        name=name,
        compiler_params=pltpu.CompilerParams(vmem_limit_bytes=limit),
        **specs,
    )


def route_body(
    counts_hbm, offsets_hbm, columns_hbm, kernels_hbm, innov_hbm, out_hbm,
    counts_s, offsets_s, columns_s, kernels_s, innov_s, sent_s, sems, out_sems,
):
    moves = (
        (counts_hbm.at[0], counts_s),
        (offsets_hbm.at[0], offsets_s),
        (columns_hbm.at[0], columns_s),
        (kernels_hbm.at[0], kernels_s),
        (innov_hbm.at[0, 0], innov_s),
    )
    copies = [pltpu.make_async_copy(source, target, sems.at[i]) for i, (source, target) in enumerate(moves)]
    for copy in copies:
        copy.start()
    for copy in copies[:4]:
        copy.wait()
    held = innov_s.shape[1]
    owners = counts_s.shape[1]
    eye = iota((owners, owners), 0) == iota((owners, owners), 1)
    offset_col = jnp.sum(jnp.where(eye, offsets_s[...].astype(F32), 0.0), axis=1, keepdims=True)
    count_col = jnp.sum(jnp.where(eye, counts_s[...].astype(F32), 0.0), axis=1, keepdims=True)
    place = iota((owners, held), 1).astype(F32) - offset_col
    place = jnp.where(place < count_col, place, -1.0)
    slot = iota((owners, CAP, held), 1).astype(F32)
    pick = jnp.where(place[:, None, :] == slot, 1.0, 0.0).reshape(owners * CAP, held).astype(BF16)
    cell = columns_s[...]
    code = (cell + 4 * ((cell * 171) >> 11) + 1).astype(F32)
    half = WIDE // 2
    line = iota((half, held), 0)
    codes = jnp.where(
        line == CODE_LANE - half,
        code,
        jnp.where(line == KERNEL_LANE - half, kernels_s[...].astype(F32), 0.0),
    ).astype(BF16)
    tail = lax.dot_general(pick, codes, (((1,), (1,)), ((), ())), preferred_element_type=F32)
    sent_s[:, half:] = tail.astype(BF16)
    copies[4].wait()
    size = pick.shape[0] // 2
    outs = []
    for part in range(2):
        rows = slice(part * size, part * size + size)
        sent = lax.dot_general(
            pick[rows], innov_s[...], (((1,), (1,)), ((), ())), preferred_element_type=F32
        ).astype(BF16)
        sent_s[rows, :half] = sent[:, :half]
        sent_s[rows, half:WIDTH] = sent[:, half:]
        span = pl.ds(part * size, size)
        outs.append(pltpu.make_async_copy(sent_s.at[span], out_hbm.at[span], out_sems.at[part]))
        outs[part].start()
    for copy in outs:
        copy.wait()


def pack_levels(tiles):
    lane = iota(tiles[0].shape, 1)
    lane = jnp.where(lane >= LEVELS, lane - LEVELS, lane)
    packed = tiles[0]
    for index in range(1, len(tiles)):
        packed = jnp.where(lane >= 4 * index, pltpu.roll(tiles[index], 4 * index, 1), packed)
    return packed


def winds_body(winds_ref, out_ref, sibling_ref, cross_ref):
    out_ref[...] = jnp.zeros_like(out_ref)
    out_ref[:, :, :ROWS, : 2 * LEVELS] = winds_ref[...]
    even = lax.rem(lax.axis_index("lon"), 2) == 0
    sub = iota((8, 128), 0)
    made = []
    for tile in (1, 0):
        rows = []
        for row in range(ROWS):
            cuts = [out_ref[4 - step, row, :, :128].astype(F32)[8 * tile : 8 * tile + 8] for step in (1, 2, 3, 4)]
            parts = [jnp.where(sub < 4, cuts[i], pltpu.roll(cuts[i + 1], 4, 0)) for i in (0, 2)]
            rows.append(jnp.concatenate(parts, axis=0))
        made.append(pack_levels(rows))
    to_east, to_west = made
    sibling_ref[...] = jnp.where(even, to_east, to_west).astype(BF16)
    cross_ref[...] = jnp.where(even, to_west, to_east).astype(BF16)


def edge_winds(from_cross, from_sibling, row):
    even = lax.rem(lax.axis_index("lon"), 2) == 0
    sibling = from_sibling[...].astype(F32)
    cross = from_cross[...].astype(F32)
    sides = []
    for side in (jnp.where(even, sibling, cross), jnp.where(even, cross, sibling)):
        if row:
            side = pltpu.roll(side, 128 - 4 * row, 1)
        first, second = side[0:8], side[8:16]
        sides.append({1: pltpu.roll(first, 4, 0), 2: first, 3: pltpu.roll(second, 4, 0), 4: second})
    return sides


STRIP = 11
SPARE = (WIDTH - 128, WIDTH - 112)


def pieces(row):
    return pltpu.roll(row[0:8], 4, 0), row[0:8], pltpu.roll(row[8:16], 4, 0)


def with_piece(row, piece):
    sub = iota((8, row.shape[1]), 0)
    return jnp.concatenate([row[0:8], jnp.where(sub < 4, row[8:16], piece)], axis=0)


def pack_strip(lam_rows, wind_rows, east, west):
    extra = pieces(lam_rows[3])
    lane = iota((SUB, 128), 1)
    halves = []
    for index in range(3):
        packed = with_piece(lam_rows[index], extra[index])
        one, two = (pltpu.roll(wind_rows[index + 3 * i][:, 128:], SPARE[i], 1) for i in range(2))
        halves += [
            packed[:, :128],
            jnp.where(lane < SPARE[0], packed[:, 128:], jnp.where(lane < SPARE[1], one, two)),
        ]
    main = [row[:, :128] for row in wind_rows]
    extra = pieces(main[4])
    halves += [with_piece(main[index], extra[index]) for index in range(3)]
    halves += [with_piece(main[3], pack_levels(east)), with_piece(main[5], pack_levels(west))]
    return halves


def rejoin(tiles):
    first, second, third = (tile[8:16] for tile in tiles)
    sub = iota(first.shape, 0)
    return jnp.concatenate([jnp.where(sub < 4, pltpu.roll(first, 4, 0), second), pltpu.roll(third, 4, 0)], axis=0)


def unpack_strip(halves):
    tiles = [jnp.concatenate(halves[2 * i : 2 * i + 2], axis=1) for i in range(3)]
    lam_rows = tiles + [rejoin(tiles)]
    main = halves[6:10] + [rejoin(halves[6:9]), halves[10]]
    wind_rows = []
    for index in range(6):
        last = pltpu.roll(halves[2 * (index % 3) + 1], 128 - SPARE[index // 3], 1)
        wind_rows.append(jnp.concatenate([main[index], last], axis=1))
    return lam_rows, wind_rows


def force_body(
    recv_ref, table_ref, adjoint_ref, winds_ref, from_cross, from_sibling, lam_ref, north_ref, south_ref, table_s
):
    total = recv_ref.shape[0]
    nkernel = table_ref.shape[0]
    recv = recv_ref[...]
    wide = recv.astype(F32)
    pick = jnp.where((iota((8, WIDE), 1) == CODE_LANE), 1.0, 0.0).astype(BF16)
    code_line = lax.dot_general(pick, recv, (((1,), (1,)), ((), ())), preferred_element_type=F32)
    kernel_col = wide[:, KERNEL_LANE : KERNEL_LANE + 1]
    lane = iota((total, 3 * nkernel), 1)
    lane = (lane - jnp.where(lane >= nkernel, nkernel, 0) - jnp.where(lane >= 2 * nkernel, nkernel, 0)).astype(F32)
    onehot = jnp.where(kernel_col == lane, 1.0, 0.0).astype(BF16)
    table = table_ref[...]
    table_s[...] = jnp.zeros_like(table_s)
    high = table.astype(BF16)
    rest = table - high.astype(F32)
    middle = rest.astype(BF16)
    table_s[0:nkernel, :WIDTH] = high
    table_s[nkernel : 2 * nkernel, :WIDTH] = middle
    table_s[2 * nkernel :, :WIDTH] = (rest - middle.astype(F32)).astype(BF16)
    weights = jnp.dot(onehot, table_s[...], preferred_element_type=F32)
    weighted = wide * weights
    whigh = weighted.astype(BF16)
    wlow = (weighted - whigh.astype(F32)).astype(BF16)
    cell = (iota((ROWS * SUB, total), 0) + 1).astype(F32)
    scatter = jnp.where(cell == code_line[0:1, :], 1.0, 0.0).astype(BF16)
    force = jnp.dot(scatter, whigh, preferred_element_type=F32) + jnp.dot(
        scatter, wlow, preferred_element_type=F32
    )
    lam_ref[...] = force.reshape(ROWS, SUB, WIDE)
    lam_ref[:, :ROWS, :WIDTH] = lam_ref[:, :ROWS, :WIDTH] + adjoint_ref[...]
    for lower, strip in ((False, north_ref), (True, south_ref)):
        start = 0 if lower else ROWS - HALO
        wind_rows, east, west = [], [], []
        for step in (1, 2, 3):
            depth = HALO - step
            begin = 0 if lower else ROWS - depth
            for row in range(begin, begin + depth):
                wind_rows.append(winds_ref[4 - step, row].astype(F32))
                sides = edge_winds(from_cross, from_sibling, row)
                east.append(sides[0][step])
                west.append(sides[1][step])
        for index, half in enumerate(pack_strip([lam_ref[start + i] for i in range(HALO)], wind_rows, east, west)):
            strip[index] = half.astype(BF16)


WIND_FIRST = {1: 0, 2: 3, 3: 5}
EXT = ROWS + 2 * HALO


def ext_index(row):
    return row if row >= 0 else row + EXT


def wind_index(step, row):
    base = (0, 18, 34, 48)[step - 1]
    reach = HALO - step
    return base + (row if row >= 0 else row + ROWS + 2 * reach)


def edge_body(lam_ref, from_south, from_north, winds_ref, _, sibling_ref, cross_ref, lam_out, winds_out):
    south_lam, south_winds = unpack_strip([from_south[i].astype(F32) for i in range(STRIP)])
    north_lam, north_winds = unpack_strip([from_north[i].astype(F32) for i in range(STRIP)])
    even = lax.rem(lax.axis_index("lon"), 2) == 0
    sub = iota((8, WIDE), 0)
    lane = iota((8, 128), 1)
    none = jnp.zeros((SUB, WIDE), F32)
    held = {}
    for row in sorted(range(-HALO, ROWS + HALO), key=ext_index):
        own = 0 <= row < ROWS
        lam = lam_ref[row] if own else (south_lam[row + HALO] if row < 0 else north_lam[row - ROWS])
        lam_out[ext_index(row)] = lam
        wind = {}
        for step in (1, 2, 3, 4):
            reach = HALO - step
            if own:
                raw = winds_ref[4 - step, row]
                winds_out[wind_index(step, row)] = raw
                wind[step] = raw.astype(F32)
            elif -reach <= row < ROWS + reach:
                rows, at = (south_winds, row + reach) if row < 0 else (north_winds, row - ROWS)
                wind[step] = rows[WIND_FIRST[step] + at]
                winds_out[wind_index(step, row)] = wind[step].astype(BF16)
            else:
                wind[step] = none
        made = []
        for tile in (1, 0):
            cut = slice(8 * tile, 8 * tile + 8)
            upper = pltpu.roll(wind[1][cut], 4, 0)
            if tile == 1:
                rest = jnp.where(sub >= 2, wind[2][cut], pltpu.roll(wind[3][cut], 6, 0))
            else:
                rest = jnp.where(sub < 2, wind[2][cut], pltpu.roll(wind[3][cut], 2, 0))
            made.append((lam[cut], jnp.where(sub >= 4, upper, rest)))
        if ext_index(row) % 2 == 0:
            held = made
            continue
        strips = []
        for (lam_a, wind_a), (lam_b, wind_b) in zip(held, made, strict=True):
            both = jnp.where(sub < 4, lam_a, pltpu.roll(lam_b, 4, 0))
            one = pltpu.roll(wind_a[:, 128:], SPARE[0], 1)
            two = pltpu.roll(wind_b[:, 128:], SPARE[1], 1)
            last = jnp.where(lane < SPARE[0], both[:, 128:], jnp.where(lane < SPARE[1], one, two))
            upper = jnp.concatenate([both[:, :128], last], axis=1)
            lower = jnp.concatenate([wind_a[:, :128], wind_b[:, :128]], axis=1)
            strips.append(jnp.concatenate([upper, lower], axis=0))
        to_east, to_west = strips
        sibling_ref[ext_index(row) // 2] = jnp.where(even, to_east, to_west).astype(BF16)
        cross_ref[ext_index(row) // 2] = jnp.where(even, to_west, to_east).astype(BF16)


def assemble(refs, lam_s, wide_s):
    lam_ref, winds_ref, from_cross, from_sibling = refs
    even = lax.rem(lax.axis_index("lon"), 2) == 0
    sub = iota((8, WIDE), 0)
    for row in range(-HALO, ROWS + HALO):
        at = ext_index(row)
        lam = lam_ref[at]
        sibling = from_sibling[at // 2].astype(F32)
        cross = from_cross[at // 2].astype(F32)
        east = jnp.where(even, sibling, cross)
        west = jnp.where(even, cross, sibling)
        odd = at % 2
        east_lam, west_lam = east[0:8], west[0:8]
        if not odd:
            east_lam, west_lam = pltpu.roll(east_lam, 4, 0), pltpu.roll(west_lam, 4, 0)
        lam_s[at, 0:8] = lam[0:8]
        lam_s[at, 8:16] = jnp.where(sub < 4, lam[8:16], east_lam)
        lam_s[at, 16:24] = west_lam
        east_wind, west_wind = (side[8:16, 128 * odd : 128 * odd + 128] for side in (east, west))
        east_wind, west_wind = (
            jnp.concatenate([main, pltpu.roll(side[0:8, 128:], 128 - SPARE[odd], 1)], axis=1)
            for main, side in ((east_wind, east), (west_wind, west))
        )
        for step in range(1, 5):
            reach = HALO - step
            if not -reach <= row < ROWS + reach:
                continue
            place = wind_index(step, row)
            wind = winds_ref[place].astype(F32)
            ew, ww = east_wind, west_wind
            if step == 2:
                ew, ww = pltpu.roll(ew, 4, 0), pltpu.roll(ww, 4, 0)
            if step == 3:
                ew, ww = pltpu.roll(ew, 2, 0), pltpu.roll(ww, 6, 0)
            wide_s[place, 0:16] = jnp.concatenate(
                [wind[0:8], jnp.where(sub < 4, wind[8:16], ew)], axis=0
            ).astype(BF16)
            wide_s[place, 16:24] = ww.astype(BF16)


def wind_spread():
    source = iota((WIDE, 2 * WIDE), 0)
    lane = iota((WIDE, 2 * WIDE), 1)
    second = lane >= WIDE
    lane = jnp.where(second, lane - WIDE, lane)
    level = lane - jnp.where(lane >= LEVELS, LEVELS, 0) - jnp.where(lane >= 2 * LEVELS, LEVELS, 0)
    match = (source == level + jnp.where(second, LEVELS, 0)) & (lane < WIDTH)
    return jnp.where(match, 0.5, 0.0).astype(BF16)


def poles():
    lat = lax.axis_index("lat")
    has_south = jnp.where(lat > 0, 1.0, 0.0).astype(F32)
    return has_south, jnp.where(lat < lax.axis_size("lat") - 1, 1.0, 0.0).astype(F32)


def updated(mid, north, south, u, v, top, bottom):
    cols, lanes = mid.shape
    east = pltpu.roll(mid, cols - 1, 0)
    west = pltpu.roll(mid, 1, 0)
    upper = pltpu.roll(mid, lanes - 1, 1)
    if top is not None:
        upper = jnp.where(top, mid, upper)
    lower = jnp.where(bottom, mid, pltpu.roll(mid, 1, 1))
    return (
        CENTER * mid
        + u * (east - west)
        + v * (north - south)
        + HORIZ_MIX * ((east + west) + (north + south))
        + VERT_MIX * (upper + lower)
    )


def advance(lam_a, lam_b, wide_s, coef_s, field_ref):
    has_south, has_north = poles()
    cols = SUB + 8
    spread = wind_spread()
    lane = iota((cols, WIDE), 1)
    top = (lane == LEVELS - 1) | (lane == 2 * LEVELS - 1) | (lane == 3 * LEVELS - 1)
    bottom = (lane == 0) | (lane == LEVELS) | (lane == 2 * LEVELS)
    now, later = lam_a, lam_b
    for step in range(1, 5):
        reach = HALO - step
        count = ROWS + 2 * reach
        base = wind_index(step, 0)
        lhs = wide_s[base : base + count].reshape(count * cols, WIDE)
        coef_s[base : base + count] = jnp.dot(lhs, spread, preferred_element_type=F32).reshape(count, cols, 2 * WIDE)
        for row in range(-reach, ROWS + reach):
            place = wind_index(step, row)
            new = updated(
                now[ext_index(row)], now[ext_index(row + 1)], now[ext_index(row - 1)],
                coef_s[place, :, :WIDE], coef_s[place, :, WIDE:], top, bottom,
            )
            if row < 0:
                new = new * has_south
            if row >= ROWS:
                new = new * has_north
            if step < 4:
                later[ext_index(row)] = new
            else:
                field_ref[row] = new[:ROWS, :WIDTH]
        now, later = later, now


GROUP = EXT // 4
SPECIES_LANES = 8


def low_levels(tile):
    lane = iota((8, 128), 1)
    first = tile[:, :128]
    low = jnp.where(
        lane < SPECIES_LANES,
        first,
        jnp.where(lane < 2 * SPECIES_LANES, pltpu.roll(first, 128 - LEVELS + SPECIES_LANES, 1), tile[:, 128:]),
    )
    return jnp.where(lane < SPECIES * SPECIES_LANES, low, 0.0)


def assemble_low(refs, lam_s, wide_s):
    lam_ref, from_south, from_north, winds_ref, from_cross, from_sibling = refs
    sub = iota((8, 128), 0)
    halos = []
    for strip in (from_south, from_north):
        halves = [strip[i].astype(F32) for i in range(STRIP)]
        halos.append((*unpack_strip(halves), halves[9][8:16], halves[10][8:16]))
    held = [[jnp.zeros((8, 128), F32)] * 2 for _ in range(GROUP)]
    for row in range(-HALO, ROWS + HALO):
        own = 0 <= row < ROWS
        group, at = divmod(row + HALO, GROUP)
        if own:
            lam = lam_ref[row]
            sides = edge_winds(from_cross, from_sibling, row)
        else:
            lam_rows, wind_rows, east, west = halos[0 if row < 0 else 1]
            lam = lam_rows[row + HALO if row < 0 else row - ROWS]
        for tile in range(2):
            low = low_levels(lam[8 * tile : 8 * tile + 8])
            held[at][tile] = held[at][tile] + (pltpu.roll(low, 32 * group, 1) if group else low)
        lanes = slice(128 * group, 128 * group + 128)
        for step in range(1, 5):
            reach = HALO - step
            place = (step - 1) * GROUP + at
            if not -reach <= row < ROWS + reach:
                wide_s[place, :, lanes] = jnp.zeros((SUB + 8, 128), BF16)
                continue
            if own:
                wind = winds_ref[4 - step, row, :, :128].astype(F32)
                east_wind, west_wind = sides[0][step], sides[1][step]
            else:
                index = WIND_FIRST[step] + (row + reach if row < 0 else row - ROWS)
                wind = wind_rows[index][:, :128]
                east_wind, west_wind = (pltpu.roll(side, 128 - 4 * index, 1) if index else side for side in (east, west))
            wide_s[place, 0:16, lanes] = jnp.concatenate(
                [wind[0:8], jnp.where(sub < 4, wind[8:16], east_wind)], axis=0
            ).astype(BF16)
            wide_s[place, 16:24, lanes] = west_wind.astype(BF16)
    for at in range(GROUP):
        lam_s[at, 0:8] = held[at][0]
        lam_s[at, 8:16] = jnp.where(sub < 4, held[at][1], 0.0)
        lam_s[at, 16:24] = jnp.zeros((8, 128), F32)


def low_spread():
    source = iota((4 * 128, 2 * 128), 0)
    lane = iota((4 * 128, 2 * 128), 1)
    level = lane & (SPECIES_LANES - 1)
    wanted = ((lane & 127) >> 5) * 128 + level + jnp.where(lane >= 128, LEVELS, 0)
    match = (source == wanted) & (level < 4) & ((lane & 31) < SPECIES * SPECIES_LANES)
    return jnp.where(match, 0.5, 0.0).astype(BF16)


def advance_low(lam_a, lam_b, wide_s, coef_s, acc_s):
    has_south, has_north = poles()
    cols = SUB + 8
    spread = low_spread()
    lane = iota((cols, 128), 1)
    bottom = (lane & (SPECIES_LANES - 1)) == 0
    lhs = wide_s[...].reshape(4 * GROUP * cols, 4 * 128)
    coef_s[...] = jnp.dot(lhs, spread, preferred_element_type=F32).reshape(4 * GROUP, cols, 2 * 128)
    now, later = lam_a, lam_b
    for step in range(1, 5):
        for at in range(GROUP):
            place = (step - 1) * GROUP + at
            north = now[at + 1] if at < GROUP - 1 else pltpu.roll(now[0], 96, 1)
            south = now[at - 1] if at else pltpu.roll(now[GROUP - 1], 32, 1)
            new = updated(now[at], north, south, coef_s[place, :, :128], coef_s[place, :, 128:], None, bottom)
            if at < HALO:
                new = jnp.where(lane < 32, new * has_south, new)
            if at > 0:
                new = jnp.where(lane >= 96, new * has_north, new)
            later[at] = new
            acc_s[at] = new if step == 1 else acc_s[at] + new
        now, later = later, now


LOW = WIDTH // 6


def surface_body(
    lam_ref, from_south, from_north, winds_ref, from_cross, from_sibling, _, out_ref, lam_a, lam_b, wide_s, coef_s, acc_s
):
    assemble_low((lam_ref, from_south, from_north, winds_ref, from_cross, from_sibling), lam_a, wide_s)
    advance_low(lam_a, lam_b, wide_s, coef_s, acc_s)
    lane = iota((SUB + 8, 128), 1)
    surface = jnp.zeros((SUB + 8, 128), F32)
    for row in range(ROWS):
        group, place = divmod(row + HALO, GROUP)
        held = acc_s[place]
        for species in range(SPECIES):
            at = row * SPECIES + species
            source = 32 * group + SPECIES_LANES * species
            surface = jnp.where(lane == at, pltpu.roll(held, (at - source) % 128, 1), surface)
    high = surface.astype(BF16).astype(F32)
    low = (surface - high).astype(BF16).astype(F32)
    lane = iota((8, 128), 1)
    parts = []
    for tile, last in ((0, high), (1, low)):
        cut = slice(8 * tile, 8 * tile + 8)
        second = pltpu.roll(low[cut], LOW, 1)
        third = pltpu.roll(last[16:24], 2 * LOW, 1)
        parts.append(jnp.where(lane < LOW, high[cut], jnp.where(lane < 2 * LOW, second, third)))
    block = jnp.concatenate(parts, axis=0).astype(BF16)
    for target in range(out_ref.shape[0] // SUB):
        out_ref[SUB * target : SUB * target + SUB] = block


def steps_body(lam_ref, winds_ref, from_cross, from_sibling, field_ref, lam_a, lam_b, wide_s, coef_s):
    refs = (lam_ref, winds_ref, from_cross, from_sibling)
    assemble(refs, lam_a, wide_s)
    advance(lam_a, lam_b, wide_s, coef_s, field_ref)


def correlation_body(correlation_ref, out_ref):
    total = correlation_ref.shape[1]
    length = total // ROWS * 8
    source = iota((total, length), 0)
    block = iota((total, length), 1) >> 3
    place = iota((total, length), 1) & 7
    first = source == block * ROWS + place
    second = (source == block * ROWS + 8 + place) & (place < 4)
    for index, match in enumerate((first, second)):
        pick = jnp.where(match, 1.0, 0.0).astype(BF16)
        part = jnp.dot(correlation_ref[...], pick, preferred_element_type=F32)
        part = jnp.concatenate([part, jnp.zeros((SUB - ROWS, length), F32)], axis=0)
        out_ref[SUB * index : SUB * index + SUB] = part.astype(BF16)


def gradient_body(surface_ref, correlation_ref, out_ref, blocks_s):
    blocks = surface_ref.shape[0] // SUB
    lane = iota((8, 128), 1)
    sub = iota((8, 128), 0)
    mains, easts, wests = [], [], []
    for block in range(blocks):
        both = surface_ref[SUB * block : SUB * block + SUB].astype(F32)
        whole = both + pltpu.roll(both, 128 - LOW, 1)
        mains.append(whole)
        easts.append(pltpu.roll(whole[8:16], 4, 0))
        wests.append(pltpu.roll(pltpu.roll(both[0:8] + both[8:16], 128 - 2 * LOW, 1), 4, 0))
    for pair in range(blocks // 2):
        parts = []
        for block in (2 * pair, 2 * pair + 1):
            left = mains[block][0:8] + jnp.where(sub < 4, easts[block - 1], 0.0)
            right = jnp.where(sub < 4, mains[block][8:16] + wests[(block + 1) % blocks], 0.0)
            parts.append(jnp.where(lane < 64, left, pltpu.roll(right, 64, 1)))
        blocks_s[SUB * pair : SUB * pair + SUB] = jnp.concatenate(parts, axis=0).astype(BF16)
    both = jnp.dot(correlation_ref[...], blocks_s[...], preferred_element_type=F32)
    sums = both[:SUB] + pltpu.roll(both[SUB:], 64, 1)
    result = jnp.transpose(sums)
    for row in range(ROWS):
        out_ref[row] = result[SPECIES * row : SPECIES * row + SPECIES, :ROWS]


def per_device(
    adjoint_in, stored_winds, innovations, columns, kernel_ids, counts, offsets, kernel_table, correlation
):
    lon_count = lax.axis_size("lon")
    lat_count = lax.axis_size("lat")
    shape = jax.ShapeDtypeStruct
    held = innovations.shape[2]
    sent = vmem_call(
        route_body,
        shape((lon_count * CAP, WIDE), BF16),
        [
            pltpu.VMEM((1, lon_count), jnp.int32),
            pltpu.VMEM((1, lon_count), jnp.int32),
            pltpu.VMEM((1, held), jnp.int32),
            pltpu.VMEM((1, held), jnp.int32),
            pltpu.VMEM((WIDTH, held), BF16),
            pltpu.VMEM((lon_count * CAP, WIDE), BF16),
            pltpu.SemaphoreType.DMA((5,)),
            pltpu.SemaphoreType.DMA((2,)),
        ],
        name="route",
        out_specs=pl.BlockSpec(memory_space=pltpu.HBM),
        limit=63 * 1000 * 1000,
        in_specs=[pl.BlockSpec(memory_space=pltpu.HBM)] * 5,
    )(counts, offsets, columns, kernel_ids, jnp.swapaxes(innovations, 2, 3))
    recv = lax.all_to_all(sent, "lon", split_axis=0, concat_axis=0, tiled=True)
    rim = shape((SUB, 128), BF16)
    winds, rim_sibling, rim_cross = vmem_call(
        winds_body, (shape((4, ROWS, SUB, WIDE), BF16), rim, rim), name="winds"
    )(stored_winds)
    across = [(i, (i + (1 if i % 2 else -1)) % lon_count) for i in range(lon_count)]
    within = [(i, i ^ 1) for i in range(lon_count)]
    winds_cross = lax.ppermute(rim_cross, "lon", across)
    winds_sibling = lax.ppermute(rim_sibling, "lon", within)
    turned = vmem_call(correlation_body, shape((2 * SUB, lon_count * 8), BF16), name="correlation")(correlation.T)
    strip = shape((STRIP, SUB, 128), BF16)
    lam, north, south = vmem_call(
        force_body,
        (shape((ROWS, SUB, WIDE), F32), strip, strip),
        [pltpu.VMEM((3 * kernel_table.shape[0], WIDE), BF16)],
        name="force",
    )(recv, kernel_table, adjoint_in, winds, winds_cross, winds_sibling)
    up = [(i, i + 1) for i in range(lat_count - 1)]
    down = [(i + 1, i) for i in range(lat_count - 1)]
    from_south = lax.ppermute(north, "lat", up)
    from_north = lax.ppermute(south, "lat", down)
    cols = SUB + 8
    vmem = pl.BlockSpec(memory_space=pltpu.VMEM)
    surface = vmem_call(
        surface_body,
        shape((lon_count * SUB, 128), BF16),
        [
            pltpu.VMEM((GROUP, cols, 128), F32),
            pltpu.VMEM((GROUP, cols, 128), F32),
            pltpu.VMEM((4 * GROUP, cols, 4 * 128), BF16),
            pltpu.VMEM((4 * GROUP, cols, 2 * 128), F32),
            pltpu.VMEM((GROUP, cols, 128), F32),
        ],
        name="surface",
        in_specs=[vmem] * 6 + [pl.BlockSpec(memory_space=pl.ANY)],
    )(lam, from_south, from_north, winds, winds_cross, winds_sibling, turned)
    gathered = lax.all_to_all(surface, "lon", split_axis=0, concat_axis=0, tiled=True)
    edge = shape((EXT // 2, SUB, WIDE), BF16)
    to_sibling, to_cross, lam_ext, winds_ext = vmem_call(
        edge_body,
        (edge, edge, shape((EXT, SUB, WIDE), F32), shape((60, SUB, WIDE), BF16)),
        name="edge",
        in_specs=[vmem] * 4 + [pl.BlockSpec(memory_space=pl.ANY)],
    )(lam, from_south, from_north, winds, surface)
    from_cross = lax.ppermute(to_cross, "lon", across)
    from_sibling = lax.ppermute(to_sibling, "lon", within)
    state = (lam_ext, winds_ext, from_cross, from_sibling)
    gradient = vmem_call(
        gradient_body,
        shape((ROWS, SPECIES, ROWS), F32),
        [pltpu.VMEM((lon_count * 8, 128), BF16)],
        name="gradient",
    )(gathered, turned)
    field = vmem_call(
        steps_body,
        shape((ROWS, ROWS, WIDTH), F32),
        [
            pltpu.VMEM((EXT, cols, WIDE), F32),
            pltpu.VMEM((EXT, cols, WIDE), F32),
            pltpu.VMEM((60, cols, WIDE), BF16),
            pltpu.VMEM((60, cols, 2 * WIDE), F32),
        ],
        name="steps",
    )(*state)
    return field, gradient


def solution(mesh):
    return jax.shard_map(
        per_device,
        mesh=mesh,
        in_specs=(
            P("lat", "lon", None),
            P(None, "lat", "lon", None),
            P("lat", "lon", None, None),
            P("lat", "lon", None),
            P("lat", "lon", None),
            P("lat", "lon", None),
            P("lat", "lon", None),
            P(),
            P(None, "lon"),
        ),
        out_specs=(P("lat", "lon", None), P("lat", None, "lon")),
        check_vma=False,
    )
```
